32 devices in a mesh: dp: 4 (over x, core), expert: 8 (over z, y).
Axes of the slice: x: 2, y: 2, z: 4, core: 2. Of those that a mesh axis runs over, the one named last changes fastest.
Arguments:
- hidden_states: bfloat16 [4096, 2048], P(('dp', 'expert')), may hold values from -18 to 18
- out_grad: bfloat16 [4096, 2048], P(('dp', 'expert')), may hold values from -6 to 6
- seq_lengths: int32 [4, 3], P('dp'), may hold values from 1 to 512, 1024 in all within a row
- seq_order: int32 [4, 3], P('dp'), may hold values from 0 to 2, each once within a row
- expert_routes: int32 [4096, 8], P(('dp', 'expert')), may hold values from 0 to 15, all different within a row; in each aligned block of 128 rows (0 to 127, 128 to 255, ...) at most 96 rows name the same one
- attn_gain: float32 [2048], replicated, may hold values from 0.5 to 1.5
- qkv_weight: bfloat16 [2048, 3, 2048], P('dp', None, 'expert'), may hold values from -0.125 to 0.125
- out_weight: bfloat16 [2048, 2048], P('dp', 'expert'), may hold values from -2.5 to 2.5
- query_gain: float32 [128], replicated, may hold values from 0.5 to 1.5
- key_gain: float32 [128], replicated, may hold values from 0.5 to 1.5
- ffn_gain: float32 [2048], replicated, may hold values from 0.5 to 1.5
- router_weight: bfloat16 [2048, 16], replicated, may hold values from -0.0625 to 0.0625
- expert_gate_up: bfloat16 [1024, 16, 2, 2048], P('dp', 'expert'), may hold values from -0.125 to 0.125
- expert_down: bfloat16 [1024, 16, 2048], P('dp', 'expert'), may hold values from -4 to 4
Outputs:
- output_states: bfloat16 [4096, 2048], P(('dp', 'expert'))
- input_grad: bfloat16 [4096, 2048], P(('dp', 'expert'))
- attn_gain_grad: float32 [2048], replicated
- qkv_weight_grad: float32 [2048, 3, 2048], P('dp', None, 'expert')
- out_weight_grad: float32 [2048, 2048], P('dp', 'expert')
- query_gain_grad: float32 [128], replicated
- key_gain_grad: float32 [128], replicated
- ffn_gain_grad: float32 [2048], replicated
- router_grad: float32 [2048, 16], replicated
- gate_up_grad: float32 [1024, 16, 2, 2048], P('dp', 'expert')
- down_grad: float32 [1024, 16, 2048], P('dp', 'expert')
- stream_rms: float32 [3], replicated
The draws below stay inside these ranges and needn't reach their ends.
Inputs may be any that keep to these rules, and one draw needn't show every extreme that they name: `seq_lengths`: each row holds the lengths of the 3 sequences of one data group; they sum to 1024, and the longest of each row is exactly 512. `seq_order`: each row is a permutation of 0 to 2. `expert_routes`: each row names 8 different experts; within the rows of one device no expert is named more than 96 times, and this bound is reached.
All inputs are finite; a program needn't handle non-finite values.
Results may differ from the reference program's by a relative error of at most 0.022.
Values may be sent and summed in bfloat16 or wider, within the bound.
No kernel may reach another device: no remote copies, remote signals or barrier semaphores. Data moves between devices by JAX's collectives and lax.ppermute only.
A program may use at most 320 MiB of HBM per device.

```python
import functools
import math
import jax
import jax.numpy as jnp
import numpy as np
from jax import lax

D = 2048
HEADS = 16
HEAD_DIM = 128
FF = 1024
TOP = 8
SEQS = 3
TOK_DEV = 128
GROUP = 1024
TOKENS = 4096
EXPERTS = 16
CAP = 96
LMAX = 512
N_DP = 4
N_EXPERT = 8


def draw_hidden_states(key, part):
    row_ids = jnp.arange(TOKENS, dtype=jnp.float32)
    rising = 1.0 + 2.0 * row_ids / max(TOKENS - 1, 1)
    values = jnp.clip(jax.random.normal(key, (TOKENS, D), jnp.float32), -6.0, 6.0) * rising[:, None]
    return values.astype(jnp.bfloat16)


def block_levels(key, dims, cuts, smallest, high):
    level = 1.0
    for dim, blocks in cuts:
        heights = jax.random.uniform(jax.random.fold_in(jax.random.fold_in(key, 6), dim), (blocks,), jnp.float32, smallest / len(cuts), high / len(cuts))
        level = level * jnp.repeat(jnp.exp(heights), dims[dim] // blocks).reshape((-1,) + (1,) * (len(dims) - 1 - dim))
    return level


def split_up(amount, total, bound, lean):
    portions = [(1 << 20) // math.isqrt(rank ** lean) + 1 for rank in range(2, amount + 1)]
    surplus, counts = total - bound - (amount - 1), [1] * (amount - 1)
    while surplus > 0:
        free = [i for i in range(amount - 1) if counts[i] < bound]
        pool, left = sum([portions[i] for i in free]), surplus
        for i in free:
            more = min(bound - counts[i], max(1, left * portions[i] // pool), surplus)
            counts[i] = counts[i] + more
            surplus = surplus - more
    return np.array([bound] + counts)


def uneven_parts(stream_key, amount, total, limit, slope):
    if amount == 2:
        one = jax.random.randint(stream_key, (), max(1, total - limit), min(limit, total - 1) + 1)
        return jnp.stack([one, total - one])
    sizes = jnp.asarray(split_up(amount, total, limit, slope), jnp.int32)
    pairs = (amount - 1) // 2
    giver, taker = sizes[1:1 + 2 * pairs:2], sizes[2:2 + 2 * pairs:2]
    slack = jnp.minimum(giver - 1, limit - taker)
    shifted = jax.random.randint(jax.random.fold_in(stream_key, 1), (pairs,), 0, 1 << 20) % (slack + 1)
    sizes = sizes.at[1:1 + 2 * pairs:2].set(giver - shifted).at[2:2 + 2 * pairs:2].set(taker + shifted)
    return sizes[jax.random.permutation(jax.random.fold_in(stream_key, 2), amount)]


def shared_out(rng, own, number, rows, amount, top, most, lean):
    sequence = jax.random.permutation(rng, amount)
    crowded, usual = load_shares(amount, rows * top, most, lean, True), load_shares(amount, rows * top, most, lean, False)
    places = jnp.arange(amount)

    def named(sizes, offset_by):
        used = int((sizes > 0).sum())
        fixed = max(1, used // 4)
        shifted = fixed + (places - fixed + offset_by * (used - fixed)) % max(1, amount - fixed)
        return jnp.zeros((amount,), jnp.int32).at[sequence[jnp.where(places < fixed, places, shifted)]].set(jnp.asarray(sizes, jnp.int32))

    sizes = jnp.where(number % 4 == 0, named(crowded, number // 4), named(usual, number - number // 4 - 1))
    mixed = jax.random.permutation(jax.random.fold_in(own, 3), amount)
    source_of, sink = mixed[0:amount // 2 * 2:2], mixed[1:amount // 2 * 2:2]
    margin = jnp.minimum(sizes[source_of] - 1, most - sizes[sink]) // 2
    margin = jnp.where((source_of == sequence[0]) | (sink == sequence[0]) | (sizes[sink] == 0), 0, jnp.maximum(margin, 0))
    shifted = jax.random.randint(jax.random.fold_in(own, 4), (amount // 2,), 0, 1 << 20) % (margin + 1)
    sizes = sizes.at[source_of].add(-shifted).at[sink].add(shifted)
    members = jnp.searchsorted(jnp.cumsum(sizes), jnp.arange(rows * top), side="right").astype(jnp.int32)
    table = members.reshape(top, rows).T
    table = table[jax.random.permutation(jax.random.fold_in(own, 1), rows)]
    offset_by = jax.random.randint(jax.random.fold_in(own, 2), (rows, 1), 0, top)
    return jnp.take_along_axis(table, (jnp.arange(top)[None, :] + offset_by) % top, axis=1)


def load_shares(count, total, reach, slope, full):
    loads = [(1 << 20) // math.isqrt(grade ** slope) + 1 for grade in range(1, count + 1)]
    largest = reach if full else min(reach, max(-(-total // count), total * loads[0] // sum(loads)))
    least = 1 if total - largest >= count - 1 else 0
    holding, surplus = [largest] + [least] * (count - 1), total - largest - least * (count - 1)
    while surplus > 0:
        candidates = [i for i in range(1, count) if holding[i] < largest] or [i for i in range(1, count) if holding[i] < reach]
        pool, left = sum([loads[i] for i in candidates]), surplus
        for i in candidates:
            addition = min(reach - holding[i], max(1, left * loads[i] // pool), surplus)
            holding[i] = holding[i] + addition
            surplus = surplus - addition
    return np.array(holding)


def noise(rng, shape, deviation, reach, shards=(), kind=jnp.bfloat16):
    drawn = deviation * jax.random.normal(rng, shape, jnp.float32)
    if shards:
        drawn = drawn * block_levels(rng, shape, shards, -0.22, 0.18)
    return jnp.clip(drawn, -reach, reach).astype(kind)


def setup_inputs(seed: int = 0) -> dict:
    key_of = jax.random.split(jax.random.key(seed), 15)
    hidden_states = draw_hidden_states(jax.random.fold_in(key_of[14], 71), 0)
    out_grad = noise(key_of[1], (TOKENS, D), 1.0, 6.0, ((0, 32),))
    seq_lengths = jax.vmap(lambda own: uneven_parts(own, SEQS, GROUP, LMAX, 2))(jax.random.split(key_of[2], N_DP)).reshape((N_DP, SEQS)).astype(jnp.int32)
    seq_order = jax.vmap(lambda own: jax.random.permutation(own, SEQS))(jax.random.split(key_of[3], N_DP)).reshape((N_DP, SEQS)).astype(jnp.int32)
    expert_routes_keys = jax.random.split(jax.random.fold_in(key_of[4], 1), TOKENS // TOK_DEV)
    expert_routes_turns = jax.random.permutation(jax.random.fold_in(key_of[4], 3), TOKENS // TOK_DEV)
    expert_routes = jax.vmap(lambda own, number: shared_out(jax.random.fold_in(key_of[4], 2), own, number, TOK_DEV, EXPERTS, TOP, CAP, 1))(expert_routes_keys, expert_routes_turns).reshape((TOKENS, TOP))
    attn_gain = jnp.clip(1.0 + 0.1 * jax.random.normal(key_of[5], (D,), jnp.float32), 0.5, 1.5)
    qkv_weight = noise(key_of[6], (D, 3, D), D ** -0.5, 0.125, ((0, 4), (2, 8)))
    out_weight = noise(key_of[7], (D, D), (3 * D // GROUP) ** -0.5, 2.5, ((0, 4), (1, 8)))
    query_gain = jnp.clip(1.0 + 0.1 * jax.random.normal(key_of[8], (HEAD_DIM,), jnp.float32), 0.5, 1.5)
    key_gain = jnp.clip(1.0 + 0.1 * jax.random.normal(key_of[9], (HEAD_DIM,), jnp.float32), 0.5, 1.5)
    ffn_gain = jnp.clip(1.0 + 0.1 * jax.random.normal(key_of[10], (D,), jnp.float32), 0.5, 1.5)
    router_weight = noise(key_of[11], (D, EXPERTS), (4 * D) ** -0.5, 0.0625)
    expert_gate_up = noise(key_of[12], (FF, EXPERTS, 2, D), D ** -0.5, 0.125, ((0, 4), (1, 8)))
    expert_down = noise(key_of[13], (FF, EXPERTS, D), (max(FF // 512, 1)) ** -0.5, 4.0, ((0, 4), (1, 8)))
    return {"hidden_states": hidden_states, "out_grad": out_grad, "seq_lengths": seq_lengths, "seq_order": seq_order, "expert_routes": expert_routes, "attn_gain": attn_gain, "qkv_weight": qkv_weight, "out_weight": out_weight, "query_gain": query_gain, "key_gain": key_gain, "ffn_gain": ffn_gain, "router_weight": router_weight, "expert_gate_up": expert_gate_up, "expert_down": expert_down}


eps_norm = 1e-06
rope_base = 10000.0
big_negative = -1e+30
highest = lax.Precision.HIGHEST

@jax.custom_vjp
def low(v):
    return lax.optimization_barrier(v.astype(jnp.bfloat16)).astype(jnp.float32)

@jax.custom_vjp
def low_back(v):
    return v

def low_keep(v):
    return (low(v), None)

def low_pass(kept, grad):
    return (grad,)

def back_keep(v):
    return (v, None)

def back_low(kept, grad):
    return (low(grad),)
low.defvjp(low_keep, low_pass)
low_back.defvjp(back_keep, back_low)

def rms_scale(values):
    return values * lax.rsqrt(lax.optimization_barrier(jnp.mean(values * values, axis=-1, keepdims=True)) + eps_norm)

def seq_layout(lengths, seq_order, row_count):
    seq_count = lengths.shape[0]
    picked_seq = seq_order[:, None] == jnp.arange(seq_count, dtype=jnp.int32)[None, :]
    ordered = lax.optimization_barrier(jnp.sum(jnp.where(picked_seq, lengths[None, :], 0), axis=1)).astype(jnp.int32)
    seq_ends = jnp.cumsum(ordered).astype(jnp.int32)
    starts = seq_ends - ordered
    places = jnp.arange(row_count, dtype=jnp.int32)
    segment = lax.optimization_barrier(jnp.sum((places[:, None] >= seq_ends[None, :]).astype(jnp.int32), axis=1))
    member = segment[:, None] == jnp.arange(seq_count, dtype=jnp.int32)[None, :]
    position = places - lax.optimization_barrier(jnp.sum(jnp.where(member, starts[None, :], 0), axis=1)).astype(jnp.int32)
    return (segment, position)

def rope_tables(position, head_dim):
    half_dim = head_dim // 2
    inv_freq = rope_base ** (-(jnp.arange(half_dim, dtype=jnp.float32) * 2.0 / head_dim))
    angles = position.astype(jnp.float32)[:, None] * inv_freq[None, :]
    return (jnp.cos(angles), jnp.sin(angles))

def rotate(values, cos_rows, sin_rows):
    half_dim = values.shape[-1] // 2
    lead_half = values[..., :half_dim]
    tail_half = values[..., half_dim:]
    cos_part = cos_rows[:, None, :]
    sin_part = sin_rows[:, None, :]
    return jnp.concatenate([lead_half * cos_part - tail_half * sin_part, tail_half * cos_part + lead_half * sin_part], axis=-1)

def attend_group(inputs):
    query_grp, key_grp, value_grp, segment_grp = inputs
    raw_scores = jnp.einsum('qhd,khd->hqk', query_grp, key_grp, precision=highest) * HEAD_DIM ** (-0.5)
    allowed = segment_grp[:, None] == segment_grp[None, :]
    scores = jnp.where(allowed[None, :, :], low_back(raw_scores), big_negative)
    soft_probs = low(jax.nn.softmax(scores, axis=-1))
    return jnp.einsum('hqk,khd->qhd', soft_probs, value_grp, precision=highest)

def slot_table(routes_grp):
    per_device = routes_grp.reshape(N_EXPERT, TOK_DEV * TOP)
    route_hits = (per_device[:, :, None] == jnp.arange(EXPERTS, dtype=jnp.int32)[None, None, :]).astype(jnp.int32)
    route_rank = jnp.cumsum(route_hits, axis=1).astype(jnp.int32) - 1
    slot_of = lax.optimization_barrier(jnp.sum(route_rank * route_hits, axis=2)).astype(jnp.int32)
    device_ids = jnp.arange(N_EXPERT, dtype=jnp.int32)[:, None]
    places = per_device * (N_EXPERT * CAP) + device_ids * CAP + slot_of
    token_ids = device_ids * TOK_DEV + jnp.arange(TOK_DEV * TOP, dtype=jnp.int32)[None, :] // TOP
    owners = jnp.zeros((EXPERTS * N_EXPERT * CAP,), jnp.int32).at[places.reshape(-1)].set(token_ids.reshape(-1) + 1)
    return owners.reshape(EXPERTS, N_EXPERT * CAP)

def reference(hidden_states, out_grad, seq_lengths, seq_order, expert_routes, attn_gain, qkv_weight, out_weight, query_gain, key_gain, ffn_gain, router_weight, expert_gate_up, expert_down):
    group_rows = TOK_DEV * N_EXPERT
    segment, position = jax.vmap(functools.partial(seq_layout, row_count=group_rows))(seq_lengths, seq_order)
    cos_rows, sin_rows = rope_tables(position.reshape(-1), HEAD_DIM)
    tables = jax.vmap(slot_table)(expert_routes.reshape(N_DP, group_rows, TOP))

    def forward(states, gain_attn, weight_qkv, weight_out, gain_query, gain_key, gain_ffn, weight_router, gate_up, down_proj):
        attn_in = low(rms_scale(states) * gain_attn)
        projected = low_back(jnp.einsum('td,dcf->tcf', attn_in, weight_qkv, precision=highest))
        head_proj = projected.reshape(TOKENS, 3, HEADS, HEAD_DIM)
        query_rows = low(rotate(rms_scale(head_proj[:, 0]) * gain_query, cos_rows, sin_rows))
        key_rows = low(rotate(rms_scale(head_proj[:, 1]) * gain_key, cos_rows, sin_rows))
        value_rows = low(head_proj[:, 2])
        shape_grp = (N_DP, group_rows, HEADS, HEAD_DIM)
        attended = lax.map(jax.checkpoint(attend_group), (query_rows.reshape(shape_grp), key_rows.reshape(shape_grp), value_rows.reshape(shape_grp), segment))
        attended = low(low_back(attended.reshape(TOKENS, D)))
        branch = low_back(jnp.dot(attended, weight_out.T, precision=highest))
        mixed_rows = states + branch
        ffn_in = low(rms_scale(mixed_rows) * gain_ffn)
        logits = low_back(jnp.dot(ffn_in, weight_router, precision=highest))
        router = jax.nn.softmax(logits, axis=-1)

        def group_moe(inputs):
            ffn_grp, router_grp, owners = inputs
            slot_live = (owners > 0).astype(jnp.float32)
            slot_rows = jnp.maximum(owners - 1, 0).astype(jnp.int32)
            rows_in = low_back(ffn_grp[slot_rows]) * slot_live[..., None]
            pre_act = low_back(jnp.einsum('esd,fekd->eskf', rows_in, gate_up, precision=highest))
            activated = low(jax.nn.silu(pre_act[:, :, 0]) * pre_act[:, :, 1])
            expert_out = low(low_back(jnp.einsum('esf,fed->esd', activated, down_proj, precision=highest)))
            gate_vals = router_grp[slot_rows, jnp.arange(EXPERTS, dtype=jnp.int32)[:, None]] * slot_live
            weighted = expert_out * gate_vals[..., None]
            return jnp.zeros((group_rows, D), jnp.float32).at[slot_rows.reshape(-1)].add(weighted.reshape(-1, D))
        moe_out = lax.map(jax.checkpoint(group_moe), (ffn_in.reshape(N_DP, group_rows, D), router.reshape(N_DP, group_rows, EXPERTS), tables)).reshape(TOKENS, D)
        return (mixed_rows + moe_out, branch, moe_out)
    primals = (hidden_states.astype(jnp.float32), attn_gain.astype(jnp.float32), qkv_weight.astype(jnp.float32), out_weight.astype(jnp.float32), query_gain.astype(jnp.float32), key_gain.astype(jnp.float32), ffn_gain.astype(jnp.float32), router_weight.astype(jnp.float32), expert_gate_up.astype(jnp.float32), expert_down.astype(jnp.float32))
    (output, branch, moe_out), pullback = jax.vjp(forward, *primals)
    gradients = pullback((out_grad.astype(jnp.float32), jnp.zeros_like(branch), jnp.zeros_like(moe_out)))
    square_sums = jnp.stack([jnp.sum(output * output), jnp.sum(branch * branch), jnp.sum(moe_out * moe_out)])
    stream_rms = jnp.sqrt(square_sums / (TOKENS * D))
    return (output.astype(jnp.bfloat16), gradients[0].astype(jnp.bfloat16), gradients[1], gradients[2], gradients[3], gradients[4], gradients[5], gradients[6], gradients[7], gradients[8], gradients[9], stream_rms)
```

```python
import functools

import jax
import jax.numpy as jnp
from jax import lax
from jax.experimental import pallas as pl
from jax.experimental.pallas import tpu as pltpu
from jax.sharding import PartitionSpec as P

eps_norm = 1e-06
rope_base = 10000.0
big_negative = -1e30
bf16 = jnp.bfloat16
f32 = jnp.float32


def expert_ring(count):
    nz = 4
    ny = count // nz
    walk = [(z, 0) for z in range(nz)]
    for z in range(nz - 1, -1, -1):
        ys = range(1, ny) if (nz - 1 - z) % 2 == 0 else range(ny - 1, 0, -1)
        walk += [(z, y) for y in ys]
    return [z * ny + y for z, y in walk]


def dot(a, b, dims):
    return lax.dot_general(a, b, (dims, ((), ())), preferred_element_type=f32)


class Ring:
    def __init__(self, count):
        self.count = count
        self.order = expert_ring(count)
        n = count
        self.down = [(self.order[(i + 1) % n], self.order[i]) for i in range(n)]
        self.up = [(self.order[i], self.order[(i + 1) % n]) for i in range(n)]
        place = [0] * n
        for i, m in enumerate(self.order):
            place[m] = i
        me = lax.axis_index("expert")
        self.me = me
        self.pos = jnp.array(place, jnp.int32)[me]
        ids = jnp.arange(n, dtype=jnp.int32)
        places = (self.pos + jnp.array(slot_order(n), jnp.int32)) % n
        table = jnp.array(self.order, jnp.int32)
        self.members = jnp.sum(jnp.where(places[:, None] == ids[None, :], table[None, :], 0), axis=1)

    def send(self, x, way):
        return lax.ppermute(x, "expert", way)

    def gather(self, own):
        n = self.count
        half = own.shape[0] // 2
        slots = [None] * n
        slots[0] = own
        ahead = behind = own
        for s in range(1, n // 2):
            ahead = self.send(ahead, self.down)
            behind = self.send(behind, self.up)
            slots[s] = ahead
            slots[n - s] = behind
        slots[n // 2] = jnp.concatenate(
            [self.send(ahead[:half], self.down), self.send(behind[half:], self.up)], axis=0
        )
        return slots

    def reduce(self, parts):
        n = self.count
        far = parts[n // 2]
        half = far.shape[0] // 2
        fwd, back = far[:half].astype(bf16), far[half:].astype(bf16)
        for s in range(n // 2 - 1, -1, -1):
            fwd = self.send(fwd, self.up)
            back = self.send(back, self.down)
            if s == 0:
                break
            a, b = parts[s].astype(f32), parts[n - s].astype(f32)
            if s == n // 2 - 1:
                fwd = jnp.concatenate([a[:half] + fwd.astype(f32), a[half:]], axis=0)
                back = jnp.concatenate([b[:half], b[half:] + back.astype(f32)], axis=0)
            else:
                fwd = a + fwd.astype(f32)
                back = b + back.astype(f32)
            fwd, back = fwd.astype(bf16), back.astype(bf16)
        return parts[0].astype(f32) + fwd.astype(f32) + back.astype(f32)


class Chips:
    def __init__(self, count):
        self.steps = count // 2
        self.swap = [(i, i ^ 1) for i in range(count)]

    def other_core(self, x):
        return lax.ppermute(x, "dp", self.swap)

    def from_ahead(self, x, step):
        n = self.steps
        return lax.ppermute(
            x, "dp", [(((i // 2 + step) % n) * 2 + i % 2, i) for i in range(2 * n)]
        )

    def to_ahead(self, x, step):
        n = self.steps
        return lax.ppermute(
            x, "dp", [(i, ((i // 2 + step) % n) * 2 + i % 2) for i in range(2 * n)]
        )

    def gather(self, own):
        blocks = []
        for step in range(self.steps):
            block = own if step == 0 else self.from_ahead(own, step)
            blocks += [block, self.other_core(block)]
        return blocks

    def reduce(self, term):
        total = None
        for step in range(self.steps - 1, -1, -1):
            theirs = self.other_core(term(2 * step + 1).astype(bf16)).astype(f32)
            mine = term(2 * step) + theirs
            if step:
                mine = self.to_ahead(mine.astype(bf16), step).astype(f32)
            total = mine if total is None else total + mine
        return total


def expert_kernel(
    steps,
    num_experts,
    f_ref,
    h_ref,
    mask_ref,
    sel_ref,
    wr_ref,
    w_ref,
    *refs,
):
    gc_ref, gp_ref, ga_ref, gl_ref, acc, router, gate_sums = refs[-7:]
    step = pl.program_id(0)
    experts_dev = sel_ref.shape[0]
    ff_tile = w_ref.shape[3]
    rows_in = f_ref[...]

    @pl.when(step == 0)
    def _():
        logits = jnp.dot(rows_in, wr_ref[...], preferred_element_type=f32)
        lane = lax.broadcasted_iota(jnp.int32, logits.shape, 1)
        logits = jnp.where(lane < num_experts, logits, big_negative)
        exps = jnp.exp(logits - jnp.max(logits, axis=-1, keepdims=True))
        router[...] = exps / jnp.sum(exps, axis=-1, keepdims=True)
        gate_sums[...] = jnp.zeros_like(gate_sums)
        acc[...] = jnp.zeros_like(acc)

    lanes = sel_ref[pl.ds(step % experts_dev, 1), :] * mask_ref[...].astype(f32)
    gate = jnp.sum(router[...] * lanes, axis=-1, keepdims=True)
    weight_gate, weight_up = w_ref[0, 0, 0], w_ref[0, 0, 1]
    gate_pre = dot(rows_in, weight_gate, ((1,), (1,)))
    up_pre = dot(rows_in, weight_up, ((1,), (1,)))
    back_hidden = h_ref[...]
    sigmoid_gate = 1.0 / (1.0 + jnp.exp(-gate_pre))
    silu_gate = gate_pre * sigmoid_gate
    act = silu_gate * up_pre
    gate_sums[...] += lanes * jnp.sum(act * back_hidden, axis=-1, keepdims=True)
    grad_hidden = back_hidden * gate
    grad_gate = grad_hidden * up_pre * sigmoid_gate * (1.0 + gate_pre * (1.0 - sigmoid_gate))
    grad_gate = grad_gate.astype(bf16)
    grad_up = (grad_hidden * silu_gate).astype(bf16)
    gp_ref[:, :ff_tile] = grad_gate
    gp_ref[:, ff_tile:] = grad_up
    ga_ref[...] = (act * gate).astype(bf16)
    acc[...] += jnp.dot(grad_gate, weight_gate, preferred_element_type=f32) + jnp.dot(
        grad_up, weight_up, preferred_element_type=f32
    )

    @pl.when(step == steps - 1)
    def _():
        sums = gate_sums[...]
        inner = jnp.sum(router[...] * sums, axis=-1, keepdims=True)
        grad_logits = (router[...] * (sums - inner)).astype(bf16)
        gl_ref[...] = grad_logits
        total = acc[...] + dot(grad_logits, wr_ref[...], ((1,), (1,)))
        gc_ref[...] = total.astype(bf16)


def expert_chunk(index, chunks, num_experts, f, hidden, mask, select, router, weights, kept):
    blocks, experts_dev, _, ff_tile, width = weights.shape
    steps = blocks * experts_dev
    rows = f.shape[0]
    whole = pl.BlockSpec(memory_space=pltpu.VMEM)
    in_specs = [
        whole,
        pl.BlockSpec((rows, ff_tile), lambda j: (index, j)),
        pl.BlockSpec((rows, 128), lambda j: (index, 0)),
        whole,
        whole,
        pl.BlockSpec(
            (1, 1, 2, ff_tile, width), lambda j: (j // experts_dev, j % experts_dev, 0, 0, 0)
        ),
    ]
    args = [f, hidden, mask, select, router, weights]
    aliases = {}
    if kept is not None:
        in_specs += [pl.BlockSpec(memory_space=pl.ANY)] * 2
        aliases = {len(args): 1, len(args) + 1: 2}
        args += list(kept)
    total = rows * chunks
    return pl.pallas_call(
        functools.partial(expert_kernel, steps, num_experts),
        grid=(steps,),
        in_specs=in_specs,
        out_specs=[
            pl.BlockSpec((rows, width), lambda j: (0, 0)),
            pl.BlockSpec((rows, 2 * ff_tile), lambda j: (index, j)),
            pl.BlockSpec((rows, ff_tile), lambda j: (index, j)),
            pl.BlockSpec((rows, 128), lambda j: (0, 0)),
        ],
        out_shape=[
            jax.ShapeDtypeStruct((rows, width), bf16),
            jax.ShapeDtypeStruct((total, 2 * ff_tile * steps), bf16),
            jax.ShapeDtypeStruct((total, ff_tile * steps), bf16),
            jax.ShapeDtypeStruct((rows, 128), bf16),
        ],
        scratch_shapes=[
            pltpu.VMEM((rows, width), f32),
            pltpu.VMEM((rows, 128), f32),
            pltpu.VMEM((rows, 128), f32),
        ],
        input_output_aliases=aliases,
        compiler_params=pltpu.CompilerParams(vmem_limit_bytes=48 << 20),
        cost_estimate=pl.CostEstimate(
            flops=8 * rows * ff_tile * steps * width,
            bytes_accessed=4 * ff_tile * steps * width,
            transcendentals=0,
        ),
    )(*args)


def all_sum(x):
    for axis in ("dp", "expert"):
        n = lax.axis_size(axis)
        bit = 1
        while bit < n:
            x = x + lax.ppermute(x, axis, [(i, i ^ bit) for i in range(n)])
            bit *= 2
    return x


def slot_order(n):
    return [k for i in range(n // 2) for k in ((n - i) % n, i + 1)]


def in_order(slots):
    return jnp.concatenate([slots[k] for k in slot_order(len(slots))], axis=0)


def after(x, *others):
    return lax.optimization_barrier((x, *others))[0]


def rms_scale(values):
    return lax.rsqrt(jnp.mean(values * values, axis=-1, keepdims=True) + eps_norm)


def norm_back(grad_out, norm_gain, normed, row_scale):
    scaled = grad_out * norm_gain
    inner_mean = jnp.mean(normed * scaled, axis=-1, keepdims=True)
    return row_scale * (scaled - normed * inner_mean)


def seq_layout(lengths, seq_order, places):
    seq_count = lengths.shape[0]
    ids = jnp.arange(seq_count, dtype=jnp.int32)
    picked_seq = seq_order[:, None] == ids[None, :]
    ordered = jnp.sum(jnp.where(picked_seq, lengths[None, :], 0), axis=1)
    upto = ids[:, None] >= ids[None, :]
    seq_ends = jnp.sum(jnp.where(upto, ordered[None, :], 0), axis=1)
    starts = seq_ends - ordered
    segment = jnp.sum((places[:, None] >= seq_ends[None, :]).astype(jnp.int32), axis=1)
    member = segment[:, None] == ids[None, :]
    position = places - jnp.sum(jnp.where(member, starts[None, :], 0), axis=1)
    return (segment, position)


def rope_tables(position, head_dim):
    half_dim = head_dim // 2
    inv_freq = rope_base ** (-(jnp.arange(half_dim, dtype=f32) * 2.0 / head_dim))
    angles = position.astype(f32)[:, None] * inv_freq[None, :]
    return (jnp.cos(angles), jnp.sin(angles))


def rotate(values, cos_rows, sin_rows):
    half_dim = values.shape[-1] // 2
    a, b = values[..., :half_dim], values[..., half_dim:]
    return jnp.concatenate([a * cos_rows - b * sin_rows, b * cos_rows + a * sin_rows], axis=-1)


def rotate_back(grad_out, cos_rows, sin_rows):
    return rotate(grad_out, cos_rows, -sin_rows)


def attend(query, key, value, segment, scaling):
    scores = jnp.einsum("hqd,hkd->hqk", query, key, preferred_element_type=f32) * scaling
    allowed = segment[:, None] == segment[None, :]
    scores = jnp.where(allowed[None], scores, big_negative)
    row_max = jnp.max(scores, axis=-1, keepdims=True)
    exp_scores = jnp.exp(scores - row_max)
    row_sum = jnp.sum(exp_scores, axis=-1, keepdims=True)
    probs = (exp_scores / row_sum).astype(bf16)
    attended = jnp.einsum("hqk,hkd->hqd", probs, value, preferred_element_type=f32)
    return attended, row_max + jnp.log(row_sum)


def attend_back(query, key, value, grad, segment, log_sums, scaling):
    scores = jnp.einsum("hqd,hkd->hqk", query, key, preferred_element_type=f32) * scaling
    allowed = segment[:, None] == segment[None, :]
    scores = jnp.where(allowed[None], scores, big_negative)
    probs = jnp.exp(scores - log_sums)
    grad_probs = jnp.einsum("hqd,hkd->hqk", grad, value, preferred_element_type=f32)
    inner = jnp.sum(probs * grad_probs, axis=-1, keepdims=True)
    grad_scores = (probs * (grad_probs - inner)).astype(bf16)
    grad_query = jnp.einsum("hqk,hkd->hqd", grad_scores, key, preferred_element_type=f32) * scaling
    grad_key = jnp.einsum("hqk,hqd->hkd", grad_scores, query, preferred_element_type=f32) * scaling
    grad_value = jnp.einsum("hqk,hqd->hkd", probs.astype(bf16), grad, preferred_element_type=f32)
    return grad_query, grad_key, grad_value


def on_device(
    hidden_states,
    out_grad,
    seq_lengths,
    seq_order,
    expert_routes,
    attn_gain,
    qkv_weight,
    out_weight,
    query_gain,
    key_gain,
    ffn_gain,
    router_weight,
    expert_gate_up,
    expert_down,
):
    tok_rows, width = hidden_states.shape
    head_dim = query_gain.shape[0]
    ff_dev, experts_dev = expert_gate_up.shape[:2]
    n_dp = lax.axis_size("dp")
    n_exp = lax.axis_size("expert")
    ff = ff_dev * n_dp
    num_experts = experts_dev * n_exp
    scaling = head_dim ** (-0.5)
    ring = Ring(n_exp)
    rows = tok_rows * n_exp

    chips = Chips(n_dp)
    qkv_full = lax.all_gather(qkv_weight.transpose(1, 0, 2), "dp", axis=1, tiled=True)
    out_full = lax.all_gather(out_weight, "dp", axis=0, tiled=True)
    local_width = out_full.shape[1]
    heads = local_width // head_dim

    states_slots = ring.gather(hidden_states)
    states_all = in_order(states_slots).astype(f32)
    attn_scale = rms_scale(states_all)
    attn_normed = states_all * attn_scale
    features = (attn_normed * attn_gain).astype(bf16)

    gu_blocks = chips.gather(after(expert_gate_up, states_slots[1]).transpose(1, 2, 0, 3))
    gu_all = jnp.stack(gu_blocks)
    down_blocks = chips.gather(after(expert_down, gu_blocks[2]).transpose(1, 0, 2))
    down_all = jnp.stack(down_blocks).reshape(experts_dev * ff, width)

    expert_ids = jnp.arange(num_experts, dtype=jnp.int32)
    chosen = jnp.any(expert_routes[:, :, None] == expert_ids[None, None, :], axis=1)
    chosen = jnp.pad(chosen.astype(bf16), ((0, 0), (0, 128 - num_experts)))
    sent_grad = jnp.concatenate([out_grad, chosen], axis=1)
    grad_slots = ring.gather(after(sent_grad, states_slots[n_exp // 2]))
    grad_top_all = in_order([g[:, :width] for g in grad_slots])
    chosen_all = in_order([g[:, width:] for g in grad_slots])

    place = (ring.members[:, None] * tok_rows + jnp.arange(tok_rows, dtype=jnp.int32)).reshape(-1)
    segment, position = seq_layout(seq_lengths[0], seq_order[0], place)
    cos_rows, sin_rows = rope_tables(position, head_dim)

    projected = jnp.einsum("td,cdf->ctf", features, qkv_full, preferred_element_type=f32)
    head_proj = projected.reshape(3, rows, heads, head_dim).transpose(0, 2, 1, 3)
    query_scale, key_scale = rms_scale(head_proj[0]), rms_scale(head_proj[1])
    query_normed, key_normed = head_proj[0] * query_scale, head_proj[1] * key_scale
    query = rotate(query_normed * query_gain, cos_rows, sin_rows).astype(bf16)
    key = rotate(key_normed * key_gain, cos_rows, sin_rows).astype(bf16)
    value = head_proj[2].astype(bf16)
    attended, log_sums = attend(query, key, value, segment, scaling)
    attended = attended.transpose(1, 0, 2).reshape(rows, local_width).astype(bf16)
    branch_part = dot(attended, out_full, ((1,), (1,)))

    def slots_of(x):
        where = slot_order(n_exp)
        return [x[i * tok_rows : (i + 1) * tok_rows] for i in map(where.index, range(n_exp))]

    branch = ring.reduce(slots_of(branch_part))
    states = hidden_states.astype(f32)
    mixed = states + branch
    ffn_scale = rms_scale(mixed)
    ffn_normed = mixed * ffn_scale
    ffn_in = (ffn_normed * ffn_gain).astype(bf16)
    ffn_slots = ring.gather(ffn_in)
    ffn_all = in_order(ffn_slots)

    back_hidden = dot(grad_top_all, down_all, ((1,), (1,)))
    router_wide = jnp.pad(router_weight, ((0, 0), (0, 128 - num_experts)))
    lanes = jnp.arange(128, dtype=jnp.int32)
    own_ids = ring.me * experts_dev + jnp.arange(experts_dev, dtype=jnp.int32)
    select = (lanes[None, :] == own_ids[:, None]).astype(f32)
    kept = None
    grad_ffn_parts = [None] * n_exp
    logit_chunks = []
    chunks = n_exp // 2
    for i in range(chunks):
        a, b = (n_exp - i) % n_exp, i + 1
        chunk = jnp.concatenate([ffn_slots[a], ffn_slots[b]], axis=0)
        grad_chunk, grad_pre, gated_act, logit_low = expert_chunk(
            i, chunks, num_experts, chunk, back_hidden, chosen_all, select, router_wide, gu_all, kept
        )
        kept = (grad_pre, gated_act)
        grad_ffn_parts[a], grad_ffn_parts[b] = grad_chunk[:tok_rows], grad_chunk[tok_rows:]
        logit_chunks.append(logit_low)
    logit_low = jnp.concatenate(logit_chunks, axis=0)
    router_part = dot(ffn_all, logit_low, ((0,), (0,)))[:, :num_experts]
    grad_ffn = ring.reduce(grad_ffn_parts)
    moe_part = dot(gated_act, down_all, ((1,), (0,)))

    gu_cols, down_cols = experts_dev * 2 * ff_dev, experts_dev * ff_dev
    down_grad = chips.reduce(
        lambda b: dot(gated_act[:, b * down_cols : (b + 1) * down_cols], grad_top_all, ((0,), (0,)))
    ).reshape(experts_dev, ff_dev, width)
    gate_up_grad = chips.reduce(
        lambda b: dot(grad_pre[:, b * gu_cols : (b + 1) * gu_cols], ffn_all, ((0,), (0,)))
    ).reshape(experts_dev, 2, ff_dev, width)

    grad_top = out_grad.astype(f32)
    ffn_gain_part = jnp.sum(ffn_normed * grad_ffn, axis=0)
    grad_mixed = grad_top + norm_back(grad_ffn, ffn_gain, ffn_normed, ffn_scale)
    branch_slots = ring.gather(grad_mixed.astype(bf16))
    grad_rows = in_order(branch_slots)
    moe_part = after(moe_part.astype(bf16), branch_slots[n_exp // 2])
    moe = ring.reduce(slots_of(moe_part))
    output = mixed + moe

    grad_attended = dot(grad_rows, out_full, ((1,), (0,))).astype(bf16)
    grad_attended = grad_attended.reshape(rows, heads, head_dim).transpose(1, 0, 2)
    grad_query, grad_key, grad_value = attend_back(
        query, key, value, grad_attended, segment, log_sums, scaling
    )
    grad_query = rotate_back(grad_query, cos_rows, sin_rows)
    grad_key = rotate_back(grad_key, cos_rows, sin_rows)
    query_gain_part = jnp.sum(query_normed * grad_query, axis=(0, 1))
    key_gain_part = jnp.sum(key_normed * grad_key, axis=(0, 1))
    grad_query = norm_back(grad_query, query_gain, query_normed, query_scale)
    grad_key = norm_back(grad_key, key_gain, key_normed, key_scale)
    grad_proj = (
        jnp.stack([grad_query, grad_key, grad_value], axis=0)
        .astype(bf16)
        .transpose(0, 2, 1, 3)
        .reshape(3, rows, local_width)
    )
    features_part = jnp.einsum("ctf,cdf->td", grad_proj, qkv_full, preferred_element_type=f32)
    grad_features = ring.reduce(slots_of(features_part))
    qkv_term = jnp.einsum("td,ctf->cdf", features, grad_proj, preferred_element_type=f32)
    out_term = dot(grad_rows, attended, ((0,), (0,)))
    attn_sums = lax.psum_scatter(
        jnp.concatenate([qkv_term, out_term[None]], axis=0).astype(bf16),
        "dp",
        scatter_dimension=1,
        tiled=True,
    ).astype(f32)
    attn_gain_part = jnp.sum(attn_normed * features_part, axis=0)
    own_scale = rms_scale(states)
    input_grad = grad_mixed + norm_back(grad_features, attn_gain, states * own_scale, own_scale)

    squares = jnp.stack([jnp.sum(output * output), jnp.sum(branch * branch), jnp.sum(moe * moe)])
    wide = all_sum(jnp.concatenate([router_part.T, ffn_gain_part[None]], axis=0))
    small = all_sum(
        jnp.concatenate(
            [attn_gain_part, query_gain_part, key_gain_part, jnp.pad(squares, (0, 125))]
        ).reshape(-1, 128)
    ).reshape(-1)
    stream_rms = jnp.sqrt(small[width + 2 * head_dim :][:3] / (rows * n_dp * width))
    return (
        output.astype(bf16),
        input_grad.astype(bf16),
        small[:width],
        attn_sums[:3].transpose(1, 0, 2),
        attn_sums[3],
        small[width : width + head_dim],
        small[width + head_dim : width + 2 * head_dim],
        wide[num_experts],
        wide[:num_experts].T,
        gate_up_grad.transpose(2, 0, 1, 3),
        down_grad.transpose(1, 0, 2),
        stream_rms,
    )


def solution(mesh):
    in_specs = (
        P(("dp", "expert"), None),
        P(("dp", "expert"), None),
        P("dp", None),
        P("dp", None),
        P(("dp", "expert"), None),
        P(),
        P("dp", None, "expert"),
        P("dp", "expert"),
        P(),
        P(),
        P(),
        P(),
        P("dp", "expert", None, None),
        P("dp", "expert", None),
    )
    out_specs = (
        P(("dp", "expert"), None),
        P(("dp", "expert"), None),
        P(),
        P("dp", None, "expert"),
        P("dp", "expert"),
        P(),
        P(),
        P(),
        P(),
        P("dp", "expert", None, None),
        P("dp", "expert", None),
        P(),
    )
    return jax.shard_map(
        on_device, mesh=mesh, in_specs=in_specs, out_specs=out_specs, check_vma=False
    )
```

```python
import functools

import jax
import jax.numpy as jnp
from jax import lax
from jax.experimental import pallas as pl
from jax.experimental.pallas import tpu as pltpu
from jax.sharding import PartitionSpec as P

eps_norm = 1e-06
rope_base = 10000.0
big_negative = -1e30
bf16 = jnp.bfloat16
f32 = jnp.float32


def expert_ring(count):
    nz = 4
    ny = count // nz
    walk = [(z, 0) for z in range(nz)]
    for z in range(nz - 1, -1, -1):
        ys = range(1, ny) if (nz - 1 - z) % 2 == 0 else range(ny - 1, 0, -1)
        walk += [(z, y) for y in ys]
    return [z * ny + y for z, y in walk]


def dot(a, b, dims):
    return lax.dot_general(a, b, (dims, ((), ())), preferred_element_type=f32)


class Ring:
    def __init__(self, count):
        self.count = count
        self.order = expert_ring(count)
        n = count
        self.down = [(self.order[(i + 1) % n], self.order[i]) for i in range(n)]
        self.up = [(self.order[i], self.order[(i + 1) % n]) for i in range(n)]
        place = [0] * n
        for i, m in enumerate(self.order):
            place[m] = i
        me = lax.axis_index("expert")
        self.me = me
        self.pos = jnp.array(place, jnp.int32)[me]
        ids = jnp.arange(n, dtype=jnp.int32)
        places = (self.pos + jnp.array(slot_order(n), jnp.int32)) % n
        table = jnp.array(self.order, jnp.int32)
        self.members = jnp.sum(jnp.where(places[:, None] == ids[None, :], table[None, :], 0), axis=1)

    def send(self, x, way):
        return lax.ppermute(x, "expert", way)

    def gather(self, own, arrived=None, first=None, lag=2):
        n = self.count
        half = own.shape[0] // 2
        slots = [None] * n
        slots[0] = own
        ahead = behind = own
        given = {}
        for s in range(1, n // 2 + 1):
            for done in [given.get(s - lag), first if s == 2 else None]:
                if done is not None:
                    ahead, behind = tie(ahead, done), tie(behind, done)
            if s == n // 2:
                break
            ahead = self.send(ahead, self.down)
            behind = self.send(behind, self.up)
            slots[s] = ahead
            slots[n - s] = behind
            if arrived is not None and s <= n // 2 - 2:
                given[s] = arrived(s, slots)
        slots[n // 2] = jnp.concatenate(
            [self.send(ahead[:half], self.down), self.send(behind[half:], self.up)], axis=0
        )
        return slots

    def reduce(self, parts, sent=None, last=()):
        n = self.count
        far = parts[n // 2]
        half = far.shape[0] // 2
        fwd, back = far[:half].astype(bf16), far[half:].astype(bf16)
        wait = None
        for s in range(n // 2 - 1, -1, -1):
            fwd = self.send(fwd, self.up)
            back = self.send(back, self.down)
            if s == 0:
                break
            a, b = parts[s].astype(f32), parts[n - s].astype(f32)
            if wait is not None:
                a = tie(a, wait)
            wait = None
            if s == n // 2 - 1:
                fwd = jnp.concatenate([a[:half] + fwd.astype(f32), a[half:]], axis=0)
                back = jnp.concatenate([b[:half], b[half:] + back.astype(f32)], axis=0)
            else:
                fwd = a + fwd.astype(f32)
                back = b + back.astype(f32)
            fwd, back = fwd.astype(bf16), back.astype(bf16)
            wait = sent(s, back) if sent is not None else None
        total = parts[0].astype(f32)
        for ahead_of in (wait, *last):
            if ahead_of is not None:
                total = tie(total, ahead_of)
        return total + fwd.astype(f32) + back.astype(f32)


class Chips:
    def __init__(self, count):
        self.steps = count // 2
        me = lax.axis_index("dp")
        self.places = jnp.stack(
            [
                ((me // 2 + b // 2) % self.steps) * 2 + (me % 2 + b % 2) % 2
                for b in range(count)
            ]
        ).astype(jnp.int32)
        self.swap = [(i, i ^ 1) for i in range(count)]

    def other_core(self, x):
        return lax.ppermute(x, "dp", self.swap)

    def from_ahead(self, x, step):
        n = self.steps
        return lax.ppermute(
            x, "dp", [(((i // 2 + step) % n) * 2 + i % 2, i) for i in range(2 * n)]
        )

    def to_ahead(self, x, step):
        n = self.steps
        return lax.ppermute(
            x, "dp", [(i, ((i // 2 + step) % n) * 2 + i % 2) for i in range(2 * n)]
        )

    def first_half(self, own):
        ahead = [self.from_ahead(own, step) for step in range(1, self.steps)]
        return [own, self.other_core(own), *ahead]

    def second_half(self, blocks, wait):
        out = blocks[:2]
        for block in blocks[2:]:
            block = tie(block, wait)
            out += [block, self.other_core(block)]
        return out


def block_at(step, steps, experts_dev):
    block = step // experts_dev
    half = steps // experts_dev // 2
    return 2 * (block % half) + block // half


def expert_kernel(
    steps,
    num_experts,
    places,
    f_ref,
    h_ref,
    mask_ref,
    sel_ref,
    wr_ref,
    *refs,
):
    w_refs = refs[: steps // sel_ref.shape[0]]
    gc_ref, gp_ref, ga_ref, gl_ref, acc, router, gate_sums, held, sems = refs[-9:]
    step = pl.program_id(0)
    experts_dev = sel_ref.shape[0]
    ff_tile = h_ref.shape[1]
    rows_in = f_ref[...]
    now = lax.rem(step, 2)

    def fetch(target):
        for j in range(steps):

            @pl.when(target == j)
            def _():
                pltpu.make_async_copy(
                    w_refs[block_at(j, steps, experts_dev)].at[j % experts_dev],
                    held.at[j % 2],
                    sems.at[j % 2],
                ).start()

    @pl.when(step == 0)
    def _():
        fetch(step)

    fetch(step + 1)

    @pl.when(step == 0)
    def _():
        logits = jnp.dot(rows_in, wr_ref[...], preferred_element_type=f32)
        lane = lax.broadcasted_iota(jnp.int32, logits.shape, 1)
        logits = jnp.where(lane < num_experts, logits, big_negative)
        exps = jnp.exp(logits - jnp.max(logits, axis=-1, keepdims=True))
        router[...] = exps / jnp.sum(exps, axis=-1, keepdims=True)
        gate_sums[...] = jnp.zeros_like(gate_sums)
        acc[...] = jnp.zeros_like(acc)

    lanes = sel_ref[pl.ds(step % experts_dev, 1), :] * mask_ref[...].astype(f32)
    gate = jnp.sum(router[...] * lanes, axis=-1, keepdims=True)
    pltpu.make_async_copy(w_refs[0].at[0], held.at[now], sems.at[now]).wait()
    weight_gate, weight_up = held[now, 0], held[now, 1]
    gate_pre = dot(rows_in, weight_gate, ((1,), (1,)))
    up_pre = dot(rows_in, weight_up, ((1,), (1,)))
    back_hidden = h_ref[...]
    sigmoid_gate = 1.0 / (1.0 + jnp.exp(-gate_pre))
    silu_gate = gate_pre * sigmoid_gate
    act = silu_gate * up_pre
    gate_sums[...] += lanes * jnp.sum(act * back_hidden, axis=-1, keepdims=True)
    grad_hidden = back_hidden * gate
    grad_gate = grad_hidden * up_pre * sigmoid_gate * (1.0 + gate_pre * (1.0 - sigmoid_gate))
    grad_gate = grad_gate.astype(bf16)
    grad_up = (grad_hidden * silu_gate).astype(bf16)
    gp_ref[:, :ff_tile] = grad_gate
    gp_ref[:, ff_tile:] = grad_up
    ga_ref[...] = (act * gate).astype(bf16)
    acc[...] += jnp.dot(grad_gate, weight_gate, preferred_element_type=f32) + jnp.dot(
        grad_up, weight_up, preferred_element_type=f32
    )

    @pl.when(step == steps - 1)
    def _():
        sums = gate_sums[...]
        inner = jnp.sum(router[...] * sums, axis=-1, keepdims=True)
        grad_logits = (router[...] * (sums - inner)).astype(bf16)
        gl_ref[...] = grad_logits
        total = acc[...] + dot(grad_logits, wr_ref[...], ((1,), (1,)))
        gc_ref[...] = total.astype(bf16)


def expert_chunk(
    index, chunks, num_experts, places, f, hidden, mask, select, router, weights, kept
):
    experts_dev, _, ff_tile, width = weights[0].shape
    steps = len(weights) * experts_dev
    rows = f.shape[0]
    whole = pl.BlockSpec(memory_space=pltpu.VMEM)
    apart = pl.BlockSpec(memory_space=pl.ANY)

    def placed(j, places):
        return (index, places[block_at(j, steps, experts_dev)] * experts_dev + j % experts_dev)

    in_specs = [
        whole,
        pl.BlockSpec((rows, ff_tile), placed),
        pl.BlockSpec((rows, 128), lambda j, places: (index, 0)),
        whole,
        whole,
    ] + [apart] * len(weights)
    args = [places, f, hidden, mask, select, router, *weights]
    aliases = {}
    if kept is not None:
        in_specs += [apart] * 2
        aliases = {len(args) + i: 1 + i for i in range(2)}
        args += list(kept)
    total = rows * chunks
    return pl.pallas_call(
        functools.partial(expert_kernel, steps, num_experts),
        grid_spec=pltpu.PrefetchScalarGridSpec(
            num_scalar_prefetch=1,
            grid=(steps,),
            in_specs=in_specs,
            out_specs=[
                pl.BlockSpec((rows, width), lambda j, places: (0, 0)),
                pl.BlockSpec((rows, 2 * ff_tile), lambda j, places: (index, j)),
                pl.BlockSpec((rows, ff_tile), placed),
                pl.BlockSpec((rows, 128), lambda j, places: (0, 0)),
            ],
            scratch_shapes=[
                pltpu.VMEM((rows, width), f32),
                pltpu.VMEM((rows, 128), f32),
                pltpu.VMEM((rows, 128), f32),
                pltpu.VMEM((2, 2, ff_tile, width), bf16),
                pltpu.SemaphoreType.DMA((2,)),
            ],
        ),
        out_shape=[
            jax.ShapeDtypeStruct((rows, width), bf16),
            jax.ShapeDtypeStruct((total, 2 * ff_tile * steps), bf16),
            jax.ShapeDtypeStruct((total, ff_tile * steps), bf16),
            jax.ShapeDtypeStruct((rows, 128), bf16),
        ],
        input_output_aliases=aliases,
        compiler_params=pltpu.CompilerParams(vmem_limit_bytes=40 << 20),
        cost_estimate=pl.CostEstimate(
            flops=8 * rows * ff_tile * steps * width,
            bytes_accessed=4 * ff_tile * steps * width,
            transcendentals=0,
        ),
    )(*args)


def product_kernel(a_ref, b_ref, _, o_ref):
    o_ref[...] = jnp.dot(a_ref[...], b_ref[...], preferred_element_type=f32).astype(bf16)


def product(a, b, wait):
    rows, depth = a.shape
    width = b.shape[1]
    tile = min(512, rows)
    return pl.pallas_call(
        product_kernel,
        grid=(rows // tile,),
        in_specs=[
            pl.BlockSpec((tile, depth), lambda i: (i, 0)),
            pl.BlockSpec(memory_space=pltpu.VMEM),
            pl.BlockSpec(memory_space=pl.ANY),
        ],
        out_specs=pl.BlockSpec((tile, width), lambda i: (i, 0)),
        out_shape=jax.ShapeDtypeStruct((rows, width), bf16),
        compiler_params=pltpu.CompilerParams(vmem_limit_bytes=40 << 20),
        cost_estimate=pl.CostEstimate(
            flops=2 * rows * depth * width, bytes_accessed=4 * rows * depth, transcendentals=0
        ),
    )(a, b, wait)


def pair_kernel(first, block, a_ref, ap_ref, b_ref, bp_ref, x_ref, xp_ref, y_ref, yp_ref, _, o_ref):
    def product(own, peer, rows, rows_peer):
        total = dot(own[...], rows[...], ((0,), (0,))) + dot(peer[...], rows_peer[...], ((0,), (0,)))
        o_ref[...] = total.astype(o_ref.dtype)

    @pl.when(pl.program_id(0) < first)
    def _():
        product(a_ref, ap_ref, x_ref, xp_ref)

    @pl.when(pl.program_id(0) >= first)
    def _():
        product(b_ref, bp_ref, y_ref, yp_ref)


def pair_grad(
    step, block, a, peer, a_cols, x, x_peer, b, b_first, b_cols, y, y_peer, wait, dtype
):
    rows, width = x.shape
    tile = min(256, b_cols)
    first, second = a_cols // tile, b_cols // tile
    whole = pl.BlockSpec(memory_space=pltpu.VMEM)

    def a_at(j, block):
        return (0, step * first + jnp.minimum(j, first - 1))

    def b_at(j, block):
        return (0, block[0] * second + jnp.maximum(j - first, 0))

    def bp_at(j, block):
        return (0, (b_first + step) * second + jnp.maximum(j - first, 0))

    return pl.pallas_call(
        functools.partial(pair_kernel, first),
        grid_spec=pltpu.PrefetchScalarGridSpec(
            num_scalar_prefetch=1,
            grid=(first + second,),
            in_specs=[
                pl.BlockSpec((rows, tile), a_at),
                pl.BlockSpec((rows, tile), a_at),
                pl.BlockSpec((rows, tile), b_at),
                pl.BlockSpec((rows, tile), bp_at),
                whole,
                whole,
                whole,
                whole,
                pl.BlockSpec(memory_space=pl.ANY),
            ],
            out_specs=pl.BlockSpec((tile, width), lambda j, block: (j, 0)),
        ),
        out_shape=jax.ShapeDtypeStruct((a_cols + b_cols, width), dtype),
        compiler_params=pltpu.CompilerParams(vmem_limit_bytes=44 << 20),
        cost_estimate=pl.CostEstimate(
            flops=4 * rows * (a_cols + b_cols) * width,
            bytes_accessed=16 * rows * width,
            transcendentals=0,
        ),
    )(block, a, peer, b, peer, x, x_peer, y, y_peer, wait)


def all_sum(x):
    for axis in ("dp", "expert"):
        n = lax.axis_size(axis)
        bit = 1
        while bit < n:
            x = x + lax.ppermute(x, axis, [(i, i ^ bit) for i in range(n)])
            bit *= 2
    return x


def slot_order(n):
    return [k for i in range(n // 2) for k in ((n - i) % n, i + 1)]


def in_order(slots):
    return jnp.concatenate([slots[k] for k in slot_order(len(slots))], axis=0)


def tie(x, other):
    probe = other[(0,) * other.ndim]
    return x + jnp.where(probe == probe, 0.0, 1.0).astype(x.dtype)


def rms_scale(values):
    return lax.rsqrt(jnp.mean(values * values, axis=-1, keepdims=True) + eps_norm)


def norm_back(grad_out, norm_gain, normed, row_scale):
    scaled = grad_out * norm_gain
    inner_mean = jnp.mean(normed * scaled, axis=-1, keepdims=True)
    return row_scale * (scaled - normed * inner_mean)


def seq_layout(lengths, seq_order, places):
    seq_count = lengths.shape[0]
    ids = jnp.arange(seq_count, dtype=jnp.int32)
    picked_seq = seq_order[:, None] == ids[None, :]
    ordered = jnp.sum(jnp.where(picked_seq, lengths[None, :], 0), axis=1)
    upto = ids[:, None] >= ids[None, :]
    seq_ends = jnp.sum(jnp.where(upto, ordered[None, :], 0), axis=1)
    starts = seq_ends - ordered
    segment = jnp.sum((places[:, None] >= seq_ends[None, :]).astype(jnp.int32), axis=1)
    member = segment[:, None] == ids[None, :]
    position = places - jnp.sum(jnp.where(member, starts[None, :], 0), axis=1)
    return (segment, position)


def rope_tables(position, head_dim):
    half_dim = head_dim // 2
    inv_freq = rope_base ** (-(jnp.arange(half_dim, dtype=f32) * 2.0 / head_dim))
    angles = position.astype(f32)[:, None] * inv_freq[None, :]
    return (jnp.cos(angles), jnp.sin(angles))


def rotate(values, cos_rows, sin_rows):
    half_dim = values.shape[-1] // 2
    a, b = values[..., :half_dim], values[..., half_dim:]
    return jnp.concatenate([a * cos_rows - b * sin_rows, b * cos_rows + a * sin_rows], axis=-1)


def rotate_back(grad_out, cos_rows, sin_rows):
    return rotate(grad_out, cos_rows, -sin_rows)


def attend(query, key, value, segment, scaling):
    scores = jnp.einsum("hqd,hkd->hqk", query, key, preferred_element_type=f32) * scaling
    allowed = segment[:, None] == segment[None, :]
    scores = jnp.where(allowed[None], scores, big_negative)
    row_max = jnp.max(scores, axis=-1, keepdims=True)
    exp_scores = jnp.exp(scores - row_max)
    row_sum = jnp.sum(exp_scores, axis=-1, keepdims=True)
    probs = (exp_scores / row_sum).astype(bf16)
    attended = jnp.einsum("hqk,hkd->hqd", probs, value, preferred_element_type=f32)
    return attended, row_max + jnp.log(row_sum)


def attend_back(query, key, value, grad, segment, log_sums, scaling):
    scores = jnp.einsum("hqd,hkd->hqk", query, key, preferred_element_type=f32) * scaling
    allowed = segment[:, None] == segment[None, :]
    scores = jnp.where(allowed[None], scores, big_negative)
    probs = jnp.exp(scores - log_sums)
    grad_probs = jnp.einsum("hqd,hkd->hqk", grad, value, preferred_element_type=f32)
    inner = jnp.sum(probs * grad_probs, axis=-1, keepdims=True)
    grad_scores = (probs * (grad_probs - inner)).astype(bf16)
    grad_query = jnp.einsum("hqk,hkd->hqd", grad_scores, key, preferred_element_type=f32) * scaling
    grad_key = jnp.einsum("hqk,hqd->hkd", grad_scores, query, preferred_element_type=f32) * scaling
    grad_value = jnp.einsum("hqk,hqd->hkd", probs.astype(bf16), grad, preferred_element_type=f32)
    return grad_query, grad_key, grad_value


def on_device(
    hidden_states,
    out_grad,
    seq_lengths,
    seq_order,
    expert_routes,
    attn_gain,
    qkv_weight,
    out_weight,
    query_gain,
    key_gain,
    ffn_gain,
    router_weight,
    expert_gate_up,
    expert_down,
):
    tok_rows, width = hidden_states.shape
    head_dim = query_gain.shape[0]
    ff_dev, experts_dev = expert_gate_up.shape[:2]
    n_dp = lax.axis_size("dp")
    n_exp = lax.axis_size("expert")
    ff = ff_dev * n_dp
    num_experts = experts_dev * n_exp
    scaling = head_dim ** (-0.5)
    ring = Ring(n_exp)
    rows = tok_rows * n_exp

    chips = Chips(n_dp)
    qkv_full = lax.all_gather(qkv_weight.transpose(1, 0, 2), "dp", axis=1, tiled=True)
    out_full = lax.all_gather(out_weight, "dp", axis=0, tiled=True)
    local_width = out_full.shape[1]
    heads = local_width // head_dim

    states_slots = ring.gather(hidden_states)
    states_all = in_order(states_slots).astype(f32)
    attn_scale = rms_scale(states_all)
    attn_normed = states_all * attn_scale
    features = (attn_normed * attn_gain).astype(bf16)

    down_all = lax.all_gather(expert_down.transpose(1, 0, 2), "dp", axis=0)
    down_all = down_all.reshape(n_dp * experts_dev * ff_dev, width)
    gu_blocks = chips.first_half(expert_gate_up.transpose(1, 2, 0, 3))

    expert_ids = jnp.arange(num_experts, dtype=jnp.int32)
    chosen = jnp.any(expert_routes[:, :, None] == expert_ids[None, None, :], axis=1)
    chosen = jnp.pad(chosen.astype(bf16), ((0, 0), (0, 128 - num_experts)))
    sent_grad = jnp.concatenate([out_grad, chosen], axis=1)
    sent_grad = tie(sent_grad, states_slots[n_exp // 2])
    grad_slots = ring.gather(sent_grad)
    grad_top_all = in_order([g[:, :width] for g in grad_slots])
    chosen_all = in_order([g[:, width:] for g in grad_slots])
    back_hidden = dot(grad_top_all, down_all, ((1,), (1,)))

    place = (ring.members[:, None] * tok_rows + jnp.arange(tok_rows, dtype=jnp.int32)).reshape(-1)
    segment, position = seq_layout(seq_lengths[0], seq_order[0], place)
    cos_rows, sin_rows = rope_tables(position, head_dim)

    projected = jnp.einsum("td,cdf->ctf", features, qkv_full, preferred_element_type=f32)
    head_proj = projected.reshape(3, rows, heads, head_dim).transpose(0, 2, 1, 3)
    query_scale, key_scale = rms_scale(head_proj[0]), rms_scale(head_proj[1])
    query_normed, key_normed = head_proj[0] * query_scale, head_proj[1] * key_scale
    query = rotate(query_normed * query_gain, cos_rows, sin_rows)
    query = tie(query, grad_slots[1]).astype(bf16)
    key = rotate(key_normed * key_gain, cos_rows, sin_rows).astype(bf16)
    value = head_proj[2].astype(bf16)
    attended, log_sums = attend(query, key, value, segment, scaling)
    attended = attended.transpose(1, 0, 2).reshape(rows, local_width)
    attended = tie(attended, grad_slots[2]).astype(bf16)
    branch_part = dot(attended, out_full, ((1,), (1,)))

    def slots_of(x):
        where = slot_order(n_exp)
        return [x[i * tok_rows : (i + 1) * tok_rows] for i in map(where.index, range(n_exp))]

    branch = ring.reduce(slots_of(branch_part))
    states = hidden_states.astype(f32)
    mixed = states + branch
    ffn_scale = rms_scale(mixed)
    ffn_normed = mixed * ffn_scale
    ffn_in = (ffn_normed * ffn_gain).astype(bf16)
    gu_blocks = chips.second_half(gu_blocks, ffn_in)

    router_wide = jnp.pad(router_weight, ((0, 0), (0, 128 - num_experts)))
    lanes = jnp.arange(128, dtype=jnp.int32)
    own_ids = ring.me * experts_dev + jnp.arange(experts_dev, dtype=jnp.int32)
    select = (lanes[None, :] == own_ids[:, None]).astype(f32)
    chunks = n_exp // 2
    grad_ffn_parts = [None] * n_exp
    logit_chunks = [None] * chunks
    kept = [None]

    def run_chunk(i, slots):
        a, b = (n_exp - i) % n_exp, i + 1
        chunk = jnp.concatenate([slots[a], slots[b]], axis=0)
        grad_chunk, *kept_now, logit_chunks[i] = expert_chunk(
            i,
            chunks,
            num_experts,
            chips.places,
            chunk,
            back_hidden,
            chosen_all,
            select,
            router_wide,
            gu_blocks,
            kept[0],
        )
        kept[0] = tuple(kept_now)
        grad_ffn_parts[a], grad_ffn_parts[b] = grad_chunk[:tok_rows], grad_chunk[tok_rows:]
        return logit_chunks[i]

    ffn_slots = ring.gather(ffn_in, lambda s, slots: run_chunk(s - 1, slots), back_hidden, 3)
    run_chunk(chunks - 1, ffn_slots)
    run_chunk(chunks - 2, ffn_slots)
    ffn_all = in_order(ffn_slots)
    grad_pre, gated_act = kept[0]
    logit_low = jnp.concatenate(logit_chunks, axis=0)
    router_part = dot(ffn_all, logit_low, ((0,), (0,)))[:, :num_experts]

    steps = n_dp // 2
    gu_cols, down_cols = experts_dev * 2 * ff_dev, experts_dev * ff_dev
    ffn_peer, grad_peer = chips.other_core(ffn_all), chips.other_core(grad_top_all)
    pre_away = [
        grad_pre[:, (steps + s) * gu_cols : (steps + s + 1) * gu_cols] for s in range(steps)
    ]
    act_away = [
        lax.dynamic_slice_in_dim(gated_act, chips.places[2 * s + 1] * down_cols, down_cols, 1)
        for s in range(steps)
    ]
    away_peer = chips.other_core(jnp.concatenate(pre_away + act_away, axis=1))
    terms = [None] * steps
    jobs = list(range(steps - 1, -1, -1))

    def next_term(wait):
        if not jobs:
            return None
        s = jobs.pop(0)
        terms[s] = pair_grad(
            s,
            chips.places[2 * s : 2 * s + 1],
            grad_pre,
            away_peer,
            gu_cols,
            ffn_all,
            ffn_peer,
            gated_act,
            steps * gu_cols // down_cols,
            down_cols,
            grad_top_all,
            grad_peer,
            wait,
            bf16,
        )
        return terms[s]

    grad_ffn = ring.reduce(
        grad_ffn_parts, lambda s, x: next_term(x) if s == 2 else None
    )

    grad_top = out_grad.astype(f32)
    ffn_gain_part = jnp.sum(ffn_normed * grad_ffn, axis=0)
    grad_mixed = grad_top + norm_back(grad_ffn, ffn_gain, ffn_normed, ffn_scale)
    moe_made = []

    def in_gather(s, slots):
        if s == 1:
            moe_made.append(product(gated_act, down_all, slots[1]))
            return moe_made[0]
        return next_term(slots[s])

    branch_slots = ring.gather(
        grad_mixed.astype(bf16), in_gather
    )
    while jobs:
        next_term(branch_slots[n_exp // 2])
    weight_grads = terms[0].astype(f32)
    for s in range(1, steps):
        weight_grads = weight_grads + chips.to_ahead(terms[s], s).astype(f32)
    grad_rows = in_order(branch_slots)
    moe_parts = slots_of(moe_made[0])
    moe_parts[n_exp // 2] = tie(moe_parts[n_exp // 2], branch_slots[n_exp // 2])
    moe_steps = {}
    moe = ring.reduce(moe_parts, moe_steps.__setitem__)
    output = mixed + moe

    grad_attended = dot(grad_rows, out_full, ((1,), (0,))).astype(bf16)
    grad_attended = grad_attended.reshape(rows, heads, head_dim).transpose(1, 0, 2)
    grad_query, grad_key, grad_value = attend_back(
        query, key, value, grad_attended, segment, log_sums, scaling
    )
    grad_query = rotate_back(grad_query, cos_rows, sin_rows)
    grad_key = rotate_back(grad_key, cos_rows, sin_rows)
    grad_query = tie(grad_query, moe_steps[1])
    query_gain_part = jnp.sum(query_normed * grad_query, axis=(0, 1))
    key_gain_part = jnp.sum(key_normed * grad_key, axis=(0, 1))
    grad_query = norm_back(grad_query, query_gain, query_normed, query_scale)
    grad_key = norm_back(grad_key, key_gain, key_normed, key_scale)
    grad_proj = (
        jnp.stack([grad_query, grad_key, grad_value], axis=0)
        .astype(bf16)
        .transpose(0, 2, 1, 3)
        .reshape(3, rows, local_width)
    )
    features_part = jnp.einsum("ctf,cdf->td", grad_proj, qkv_full, preferred_element_type=f32)
    attn_gain_part = jnp.sum(attn_normed * features_part, axis=0)
    squares = jnp.stack([jnp.sum(output * output), jnp.sum(branch * branch), jnp.sum(moe * moe)])
    wide = all_sum(jnp.concatenate([router_part.T, ffn_gain_part[None]], axis=0))
    small = all_sum(
        jnp.concatenate(
            [attn_gain_part, query_gain_part, key_gain_part, jnp.pad(squares, (0, 125))]
        ).reshape(-1, 128)
    ).reshape(-1)
    ends = {2: weight_grads, 1: wide}
    grad_features = ring.reduce(slots_of(features_part), lambda s, x: ends.get(s), (small,))
    qkv_term = jnp.einsum("td,ctf->cdf", features, grad_proj, preferred_element_type=f32)
    out_term = dot(grad_rows, attended, ((0,), (0,)))
    attn_sums = lax.psum_scatter(
        jnp.concatenate([qkv_term, out_term[None]], axis=0).astype(bf16),
        "dp",
        scatter_dimension=1,
        tiled=True,
    ).astype(f32)
    own_scale = rms_scale(states)
    input_grad = grad_mixed + norm_back(grad_features, attn_gain, states * own_scale, own_scale)

    stream_rms = jnp.sqrt(small[width + 2 * head_dim :][:3] / (rows * n_dp * width))
    return (
        output.astype(bf16),
        input_grad.astype(bf16),
        small[:width],
        attn_sums[:3].transpose(1, 0, 2),
        attn_sums[3],
        small[width : width + head_dim],
        small[width + head_dim : width + 2 * head_dim],
        wide[num_experts],
        wide[:num_experts].T,
        weight_grads[:gu_cols].reshape(experts_dev, 2, ff_dev, width).transpose(2, 0, 1, 3),
        weight_grads[gu_cols:].reshape(experts_dev, ff_dev, width).transpose(1, 0, 2),
        stream_rms,
    )


def solution(mesh):
    in_specs = (
        P(("dp", "expert"), None),
        P(("dp", "expert"), None),
        P("dp", None),
        P("dp", None),
        P(("dp", "expert"), None),
        P(),
        P("dp", None, "expert"),
        P("dp", "expert"),
        P(),
        P(),
        P(),
        P(),
        P("dp", "expert", None, None),
        P("dp", "expert", None),
    )
    out_specs = (
        P(("dp", "expert"), None),
        P(("dp", "expert"), None),
        P(),
        P("dp", None, "expert"),
        P("dp", "expert"),
        P(),
        P(),
        P(),
        P(),
        P("dp", "expert", None, None),
        P("dp", "expert", None),
        P(),
    )
    return jax.shard_map(
        on_device, mesh=mesh, in_specs=in_specs, out_specs=out_specs, check_vma=False
    )
```

```python
import functools

import jax
import jax.numpy as jnp
from jax import lax
from jax.experimental import pallas as pl
from jax.experimental.pallas import tpu as pltpu
from jax.sharding import PartitionSpec as P

eps_norm = 1e-06
rope_base = 10000.0
big_negative = -1e30
bf16 = jnp.bfloat16
f32 = jnp.float32


def expert_ring(count):
    nz = 4
    ny = count // nz
    walk = [(z, 0) for z in range(nz)]
    for z in range(nz - 1, -1, -1):
        ys = range(1, ny) if (nz - 1 - z) % 2 == 0 else range(ny - 1, 0, -1)
        walk += [(z, y) for y in ys]
    return [z * ny + y for z, y in walk]


def dot(a, b, dims):
    return lax.dot_general(a, b, (dims, ((), ())), preferred_element_type=f32)


class Ring:
    def __init__(self, count):
        self.count = count
        self.order = expert_ring(count)
        n = count
        self.down = [(self.order[(i + 1) % n], self.order[i]) for i in range(n)]
        self.up = [(self.order[i], self.order[(i + 1) % n]) for i in range(n)]
        place = [0] * n
        for i, m in enumerate(self.order):
            place[m] = i
        me = lax.axis_index("expert")
        self.me = me
        self.pos = jnp.array(place, jnp.int32)[me]
        ids = jnp.arange(n, dtype=jnp.int32)
        places = (self.pos + jnp.array(slot_order(n), jnp.int32)) % n
        table = jnp.array(self.order, jnp.int32)
        self.members = jnp.sum(jnp.where(places[:, None] == ids[None, :], table[None, :], 0), axis=1)

    def send(self, x, way):
        return lax.ppermute(x, "expert", way)

    def gather(self, own, arrived=None, first=None, lag=2):
        n = self.count
        half = own.shape[0] // 2
        slots = [None] * n
        slots[0] = own
        ahead = behind = own
        given = {}
        for s in range(1, n // 2 + 1):
            for done in [given.get(s - lag), first if s == 2 else None]:
                if done is not None:
                    ahead, behind = tie(ahead, done), tie(behind, done)
            if s == n // 2:
                break
            ahead = self.send(ahead, self.down)
            behind = self.send(behind, self.up)
            slots[s] = ahead
            slots[n - s] = behind
            if arrived is not None and s <= n // 2 - 2:
                given[s] = arrived(s, slots)
        slots[n // 2] = jnp.concatenate(
            [self.send(ahead[:half], self.down), self.send(behind[half:], self.up)], axis=0
        )
        return slots

    def reduce(self, parts, sent=None, last=()):
        n = self.count
        far = parts[n // 2]
        half = far.shape[0] // 2
        fwd, back = far[:half].astype(bf16), far[half:].astype(bf16)
        wait = None
        for s in range(n // 2 - 1, -1, -1):
            fwd = self.send(fwd, self.up)
            back = self.send(back, self.down)
            if s == 0:
                break
            a, b = parts[s].astype(f32), parts[n - s].astype(f32)
            if wait is not None:
                a = tie(a, wait)
            wait = None
            if s == n // 2 - 1:
                fwd = jnp.concatenate([a[:half] + fwd.astype(f32), a[half:]], axis=0)
                back = jnp.concatenate([b[:half], b[half:] + back.astype(f32)], axis=0)
            else:
                fwd = a + fwd.astype(f32)
                back = b + back.astype(f32)
            fwd, back = fwd.astype(bf16), back.astype(bf16)
            wait = sent(s, back) if sent is not None else None
        total = parts[0].astype(f32)
        for ahead_of in (wait, *last):
            if ahead_of is not None:
                total = tie(total, ahead_of)
        return total + fwd.astype(f32) + back.astype(f32)


class Chips:
    def __init__(self, count):
        self.steps = count // 2
        me = lax.axis_index("dp")
        self.places = jnp.stack(
            [
                ((me // 2 + b // 2) % self.steps) * 2 + (me % 2 + b % 2) % 2
                for b in range(count)
            ]
        ).astype(jnp.int32)
        self.swap = [(i, i ^ 1) for i in range(count)]

    def other_core(self, x):
        return lax.ppermute(x, "dp", self.swap)

    def from_ahead(self, x, step):
        n = self.steps
        return lax.ppermute(
            x, "dp", [(((i // 2 + step) % n) * 2 + i % 2, i) for i in range(2 * n)]
        )

    def to_ahead(self, x, step):
        n = self.steps
        return lax.ppermute(
            x, "dp", [(i, ((i // 2 + step) % n) * 2 + i % 2) for i in range(2 * n)]
        )

    def first_half(self, own):
        ahead = [self.from_ahead(own, step) for step in range(1, self.steps)]
        return [own, self.other_core(own), *ahead]

    def second_half(self, blocks, wait):
        out = blocks[:2]
        for block in blocks[2:]:
            block = tie(block, wait)
            out += [block, self.other_core(block)]
        return out


def block_at(step, steps, experts_dev):
    block = step // experts_dev
    half = steps // experts_dev // 2
    return 2 * (block % half) + block // half


def expert_kernel(
    steps,
    num_experts,
    places,
    f_ref,
    h_ref,
    mask_ref,
    sel_ref,
    wr_ref,
    *refs,
):
    w_refs = refs[: steps // sel_ref.shape[0]]
    gc_ref, gp_ref, ga_ref, gl_ref, acc, router, gate_sums, held, sems = refs[-9:]
    step = pl.program_id(0)
    experts_dev = sel_ref.shape[0]
    ff_tile = h_ref.shape[1]
    rows_in = f_ref[...]
    now = lax.rem(step, 2)

    def fetch(target):
        for j in range(steps):

            @pl.when(target == j)
            def _():
                pltpu.make_async_copy(
                    w_refs[block_at(j, steps, experts_dev)].at[j % experts_dev],
                    held.at[j % 2],
                    sems.at[j % 2],
                ).start()

    @pl.when(step == 0)
    def _():
        fetch(step)

    fetch(step + 1)

    @pl.when(step == 0)
    def _():
        logits = jnp.dot(rows_in, wr_ref[...], preferred_element_type=f32)
        lane = lax.broadcasted_iota(jnp.int32, logits.shape, 1)
        logits = jnp.where(lane < num_experts, logits, big_negative)
        exps = jnp.exp(logits - jnp.max(logits, axis=-1, keepdims=True))
        router[...] = exps / jnp.sum(exps, axis=-1, keepdims=True)
        gate_sums[...] = jnp.zeros_like(gate_sums)
        acc[...] = jnp.zeros_like(acc)

    lanes = sel_ref[pl.ds(step % experts_dev, 1), :] * mask_ref[...].astype(f32)
    gate = jnp.sum(router[...] * lanes, axis=-1, keepdims=True)
    pltpu.make_async_copy(w_refs[0].at[0], held.at[now], sems.at[now]).wait()
    weight_gate, weight_up = held[now, 0], held[now, 1]
    gate_pre = dot(rows_in, weight_gate, ((1,), (1,)))
    up_pre = dot(rows_in, weight_up, ((1,), (1,)))
    back_hidden = h_ref[...]
    sigmoid_gate = 1.0 / (1.0 + jnp.exp(-gate_pre))
    silu_gate = gate_pre * sigmoid_gate
    act = silu_gate * up_pre
    gate_sums[...] += lanes * jnp.sum(act * back_hidden, axis=-1, keepdims=True)
    grad_hidden = back_hidden * gate
    grad_gate = grad_hidden * up_pre * sigmoid_gate * (1.0 + gate_pre * (1.0 - sigmoid_gate))
    grad_gate = grad_gate.astype(bf16)
    grad_up = (grad_hidden * silu_gate).astype(bf16)
    gp_ref[:, :ff_tile] = grad_gate
    gp_ref[:, ff_tile:] = grad_up
    ga_ref[...] = (act * gate).astype(bf16)
    acc[...] += jnp.dot(grad_gate, weight_gate, preferred_element_type=f32) + jnp.dot(
        grad_up, weight_up, preferred_element_type=f32
    )

    @pl.when(step == steps - 1)
    def _():
        sums = gate_sums[...]
        inner = jnp.sum(router[...] * sums, axis=-1, keepdims=True)
        grad_logits = (router[...] * (sums - inner)).astype(bf16)
        gl_ref[...] = grad_logits
        total = acc[...] + dot(grad_logits, wr_ref[...], ((1,), (1,)))
        gc_ref[...] = total.astype(bf16)


def expert_chunk(
    index, chunks, num_experts, places, f, hidden, mask, select, router, weights, kept
):
    experts_dev, _, ff_tile, width = weights[0].shape
    steps = len(weights) * experts_dev
    rows = f.shape[0]
    whole = pl.BlockSpec(memory_space=pltpu.VMEM)
    apart = pl.BlockSpec(memory_space=pl.ANY)

    def placed(j, places):
        return (index, places[block_at(j, steps, experts_dev)] * experts_dev + j % experts_dev)

    in_specs = [
        whole,
        pl.BlockSpec((rows, ff_tile), placed),
        pl.BlockSpec((rows, 128), lambda j, places: (index, 0)),
        whole,
        whole,
    ] + [apart] * len(weights)
    args = [places, f, hidden, mask, select, router, *weights]
    aliases = {}
    if kept is not None:
        in_specs += [apart] * 2
        aliases = {len(args) + i: 1 + i for i in range(2)}
        args += list(kept)
    total = rows * chunks
    return pl.pallas_call(
        functools.partial(expert_kernel, steps, num_experts),
        grid_spec=pltpu.PrefetchScalarGridSpec(
            num_scalar_prefetch=1,
            grid=(steps,),
            in_specs=in_specs,
            out_specs=[
                pl.BlockSpec((rows, width), lambda j, places: (0, 0)),
                pl.BlockSpec((rows, 2 * ff_tile), lambda j, places: (index, j)),
                pl.BlockSpec((rows, ff_tile), placed),
                pl.BlockSpec((rows, 128), lambda j, places: (0, 0)),
            ],
            scratch_shapes=[
                pltpu.VMEM((rows, width), f32),
                pltpu.VMEM((rows, 128), f32),
                pltpu.VMEM((rows, 128), f32),
                pltpu.VMEM((2, 2, ff_tile, width), bf16),
                pltpu.SemaphoreType.DMA((2,)),
            ],
        ),
        out_shape=[
            jax.ShapeDtypeStruct((rows, width), bf16),
            jax.ShapeDtypeStruct((total, 2 * ff_tile * steps), bf16),
            jax.ShapeDtypeStruct((total, ff_tile * steps), bf16),
            jax.ShapeDtypeStruct((rows, 128), bf16),
        ],
        input_output_aliases=aliases,
        compiler_params=pltpu.CompilerParams(vmem_limit_bytes=40 << 20),
        cost_estimate=pl.CostEstimate(
            flops=8 * rows * ff_tile * steps * width,
            bytes_accessed=4 * ff_tile * steps * width,
            transcendentals=0,
        ),
    )(*args)


def finish_kernel(experts_dev, own_ref, *refs):
    gu_ref, down_ref = refs[-2:]
    for e in range(experts_dev):
        for k in range(3):
            block = 2 * e + k if k < 2 else 2 * experts_dev + e
            total = own_ref[block].astype(f32)
            for ref in refs[:-3]:
                total = total + ref[block].astype(f32)
            if k < 2:
                gu_ref[:, e, k, :] = total
            else:
                down_ref[:, e, :] = total


def finish(terms, experts_dev, ff_dev, wait):
    width = terms[0].shape[1]
    tile = 32
    blocks = 3 * experts_dev
    return pl.pallas_call(
        functools.partial(finish_kernel, experts_dev),
        grid=(ff_dev // tile,),
        in_specs=[pl.BlockSpec((blocks, tile, width), lambda i: (0, i, 0))] * len(terms)
        + [pl.BlockSpec(memory_space=pl.ANY)],
        out_specs=[
            pl.BlockSpec((tile, experts_dev, 2, width), lambda i: (i, 0, 0, 0)),
            pl.BlockSpec((tile, experts_dev, width), lambda i: (i, 0, 0)),
        ],
        out_shape=[
            jax.ShapeDtypeStruct((ff_dev, experts_dev, 2, width), f32),
            jax.ShapeDtypeStruct((ff_dev, experts_dev, width), f32),
        ],
        compiler_params=pltpu.CompilerParams(vmem_limit_bytes=40 << 20),
        cost_estimate=pl.CostEstimate(
            flops=0, bytes_accessed=8 * blocks * ff_dev * width, transcendentals=0
        ),
    )(*[t.reshape(blocks, ff_dev, width) for t in terms], wait)


def product_kernel(a_ref, b_ref, _, o_ref):
    o_ref[...] = jnp.dot(a_ref[...], b_ref[...], preferred_element_type=f32).astype(bf16)


def product(a, b, wait):
    rows, depth = a.shape
    width = b.shape[1]
    tile = min(512, rows)
    return pl.pallas_call(
        product_kernel,
        grid=(rows // tile,),
        in_specs=[
            pl.BlockSpec((tile, depth), lambda i: (i, 0)),
            pl.BlockSpec(memory_space=pltpu.VMEM),
            pl.BlockSpec(memory_space=pl.ANY),
        ],
        out_specs=pl.BlockSpec((tile, width), lambda i: (i, 0)),
        out_shape=jax.ShapeDtypeStruct((rows, width), bf16),
        compiler_params=pltpu.CompilerParams(vmem_limit_bytes=40 << 20),
        cost_estimate=pl.CostEstimate(
            flops=2 * rows * depth * width, bytes_accessed=4 * rows * depth, transcendentals=0
        ),
    )(a, b, wait)


def pair_kernel(first, block, a_ref, ap_ref, b_ref, bp_ref, x_ref, xp_ref, y_ref, yp_ref, _, o_ref):
    def product(own, peer, rows, rows_peer):
        total = dot(own[...], rows[...], ((0,), (0,))) + dot(peer[...], rows_peer[...], ((0,), (0,)))
        o_ref[...] = total.astype(o_ref.dtype)

    @pl.when(pl.program_id(0) < first)
    def _():
        product(a_ref, ap_ref, x_ref, xp_ref)

    @pl.when(pl.program_id(0) >= first)
    def _():
        product(b_ref, bp_ref, y_ref, yp_ref)


def pair_grad(
    step, block, a, peer, a_cols, x, x_peer, b, b_first, b_cols, y, y_peer, wait, dtype
):
    rows, width = x.shape
    tile = min(256, b_cols)
    first, second = a_cols // tile, b_cols // tile
    whole = pl.BlockSpec(memory_space=pltpu.VMEM)

    def a_at(j, block):
        return (0, step * first + jnp.minimum(j, first - 1))

    def b_at(j, block):
        return (0, block[0] * second + jnp.maximum(j - first, 0))

    def bp_at(j, block):
        return (0, (b_first + step) * second + jnp.maximum(j - first, 0))

    return pl.pallas_call(
        functools.partial(pair_kernel, first),
        grid_spec=pltpu.PrefetchScalarGridSpec(
            num_scalar_prefetch=1,
            grid=(first + second,),
            in_specs=[
                pl.BlockSpec((rows, tile), a_at),
                pl.BlockSpec((rows, tile), a_at),
                pl.BlockSpec((rows, tile), b_at),
                pl.BlockSpec((rows, tile), bp_at),
                whole,
                whole,
                whole,
                whole,
                pl.BlockSpec(memory_space=pl.ANY),
            ],
            out_specs=pl.BlockSpec((tile, width), lambda j, block: (j, 0)),
        ),
        out_shape=jax.ShapeDtypeStruct((a_cols + b_cols, width), dtype),
        compiler_params=pltpu.CompilerParams(vmem_limit_bytes=44 << 20),
        cost_estimate=pl.CostEstimate(
            flops=4 * rows * (a_cols + b_cols) * width,
            bytes_accessed=16 * rows * width,
            transcendentals=0,
        ),
    )(block, a, peer, b, peer, x, x_peer, y, y_peer, wait)


def all_sum(x):
    for axis in ("dp", "expert"):
        n = lax.axis_size(axis)
        bit = 1
        while bit < n:
            x = x + lax.ppermute(x, axis, [(i, i ^ bit) for i in range(n)])
            bit *= 2
    return x


def slot_order(n):
    return [k for i in range(n // 2) for k in ((n - i) % n, i + 1)]


def in_order(slots):
    return jnp.concatenate([slots[k] for k in slot_order(len(slots))], axis=0)


def tie(x, other):
    probe = other[(0,) * other.ndim]
    return x + jnp.where(probe == probe, 0.0, 1.0).astype(x.dtype)


def rms_scale(values):
    return lax.rsqrt(jnp.mean(values * values, axis=-1, keepdims=True) + eps_norm)


def norm_back(grad_out, norm_gain, normed, row_scale):
    scaled = grad_out * norm_gain
    inner_mean = jnp.mean(normed * scaled, axis=-1, keepdims=True)
    return row_scale * (scaled - normed * inner_mean)


def seq_layout(lengths, seq_order, places):
    seq_count = lengths.shape[0]
    ids = jnp.arange(seq_count, dtype=jnp.int32)
    picked_seq = seq_order[:, None] == ids[None, :]
    ordered = jnp.sum(jnp.where(picked_seq, lengths[None, :], 0), axis=1)
    upto = ids[:, None] >= ids[None, :]
    seq_ends = jnp.sum(jnp.where(upto, ordered[None, :], 0), axis=1)
    starts = seq_ends - ordered
    segment = jnp.sum((places[:, None] >= seq_ends[None, :]).astype(jnp.int32), axis=1)
    member = segment[:, None] == ids[None, :]
    position = places - jnp.sum(jnp.where(member, starts[None, :], 0), axis=1)
    return (segment, position)


def rope_tables(position, head_dim):
    half_dim = head_dim // 2
    inv_freq = rope_base ** (-(jnp.arange(half_dim, dtype=f32) * 2.0 / head_dim))
    angles = position.astype(f32)[:, None] * inv_freq[None, :]
    return (jnp.cos(angles), jnp.sin(angles))


def rotate(values, cos_rows, sin_rows):
    half_dim = values.shape[-1] // 2
    a, b = values[..., :half_dim], values[..., half_dim:]
    return jnp.concatenate([a * cos_rows - b * sin_rows, b * cos_rows + a * sin_rows], axis=-1)


def rotate_back(grad_out, cos_rows, sin_rows):
    return rotate(grad_out, cos_rows, -sin_rows)


def attend(query, key, value, segment, scaling):
    scores = jnp.einsum("hqd,hkd->hqk", query, key, preferred_element_type=f32) * scaling
    allowed = segment[:, None] == segment[None, :]
    scores = jnp.where(allowed[None], scores, big_negative)
    row_max = jnp.max(scores, axis=-1, keepdims=True)
    exp_scores = jnp.exp(scores - row_max)
    row_sum = jnp.sum(exp_scores, axis=-1, keepdims=True)
    probs = (exp_scores / row_sum).astype(bf16)
    attended = jnp.einsum("hqk,hkd->hqd", probs, value, preferred_element_type=f32)
    return attended, row_max + jnp.log(row_sum)


def attend_back(query, key, value, grad, segment, log_sums, scaling):
    scores = jnp.einsum("hqd,hkd->hqk", query, key, preferred_element_type=f32) * scaling
    allowed = segment[:, None] == segment[None, :]
    scores = jnp.where(allowed[None], scores, big_negative)
    probs = jnp.exp(scores - log_sums)
    grad_probs = jnp.einsum("hqd,hkd->hqk", grad, value, preferred_element_type=f32)
    inner = jnp.sum(probs * grad_probs, axis=-1, keepdims=True)
    grad_scores = (probs * (grad_probs - inner)).astype(bf16)
    grad_query = jnp.einsum("hqk,hkd->hqd", grad_scores, key, preferred_element_type=f32) * scaling
    grad_key = jnp.einsum("hqk,hqd->hkd", grad_scores, query, preferred_element_type=f32) * scaling
    grad_value = jnp.einsum("hqk,hqd->hkd", probs.astype(bf16), grad, preferred_element_type=f32)
    return grad_query, grad_key, grad_value


def on_device(
    hidden_states,
    out_grad,
    seq_lengths,
    seq_order,
    expert_routes,
    attn_gain,
    qkv_weight,
    out_weight,
    query_gain,
    key_gain,
    ffn_gain,
    router_weight,
    expert_gate_up,
    expert_down,
):
    tok_rows, width = hidden_states.shape
    head_dim = query_gain.shape[0]
    ff_dev, experts_dev = expert_gate_up.shape[:2]
    n_dp = lax.axis_size("dp")
    n_exp = lax.axis_size("expert")
    ff = ff_dev * n_dp
    num_experts = experts_dev * n_exp
    scaling = head_dim ** (-0.5)
    ring = Ring(n_exp)
    rows = tok_rows * n_exp

    chips = Chips(n_dp)
    qkv_full = lax.all_gather(qkv_weight.transpose(1, 0, 2), "dp", axis=1, tiled=True)
    out_full = lax.all_gather(out_weight, "dp", axis=0, tiled=True)
    local_width = out_full.shape[1]
    heads = local_width // head_dim

    states_slots = ring.gather(hidden_states)
    states_all = in_order(states_slots).astype(f32)
    attn_scale = rms_scale(states_all)
    attn_normed = states_all * attn_scale
    features = (attn_normed * attn_gain).astype(bf16)

    down_all = lax.all_gather(expert_down.transpose(1, 0, 2), "dp", axis=0)
    down_all = down_all.reshape(n_dp * experts_dev * ff_dev, width)
    gu_blocks = chips.first_half(expert_gate_up.transpose(1, 2, 0, 3))

    expert_ids = jnp.arange(num_experts, dtype=jnp.int32)
    chosen = jnp.any(expert_routes[:, :, None] == expert_ids[None, None, :], axis=1)
    chosen = jnp.pad(chosen.astype(bf16), ((0, 0), (0, 128 - num_experts)))
    sent_grad = jnp.concatenate([out_grad, chosen], axis=1)
    place = (ring.members[:, None] * tok_rows + jnp.arange(tok_rows, dtype=jnp.int32)).reshape(-1)
    segment, position = seq_layout(seq_lengths[0], seq_order[0], place)
    cos_rows, sin_rows = rope_tables(position, head_dim)

    projected = jnp.einsum("td,cdf->ctf", features, qkv_full, preferred_element_type=f32)
    sent_grad = tie(sent_grad, states_slots[n_exp // 2])
    stages = {1: projected}
    grad_slots = ring.gather(sent_grad, lambda s, slots: stages.get(s), lag=1)
    grad_top_all = in_order([g[:, :width] for g in grad_slots])
    chosen_all = in_order([g[:, width:] for g in grad_slots])
    back_hidden = dot(grad_top_all, down_all, ((1,), (1,)))

    head_proj = projected.reshape(3, rows, heads, head_dim).transpose(0, 2, 1, 3)
    query_scale, key_scale = rms_scale(head_proj[0]), rms_scale(head_proj[1])
    query_normed, key_normed = head_proj[0] * query_scale, head_proj[1] * key_scale
    query = rotate(query_normed * query_gain, cos_rows, sin_rows)
    query = tie(query, grad_slots[1]).astype(bf16)
    key = rotate(key_normed * key_gain, cos_rows, sin_rows).astype(bf16)
    value = head_proj[2].astype(bf16)
    attended, log_sums = attend(query, key, value, segment, scaling)
    attended = attended.transpose(1, 0, 2).reshape(rows, local_width)
    attended = tie(attended, grad_slots[2]).astype(bf16)
    branch_part = dot(attended, out_full, ((1,), (1,)))

    def slots_of(x):
        where = slot_order(n_exp)
        return [x[i * tok_rows : (i + 1) * tok_rows] for i in map(where.index, range(n_exp))]

    branch = ring.reduce(slots_of(branch_part))
    states = hidden_states.astype(f32)
    mixed = states + branch
    ffn_scale = rms_scale(mixed)
    ffn_normed = mixed * ffn_scale
    ffn_in = (ffn_normed * ffn_gain).astype(bf16)
    gu_blocks = chips.second_half(gu_blocks, ffn_in)

    router_wide = jnp.pad(router_weight, ((0, 0), (0, 128 - num_experts)))
    lanes = jnp.arange(128, dtype=jnp.int32)
    own_ids = ring.me * experts_dev + jnp.arange(experts_dev, dtype=jnp.int32)
    select = (lanes[None, :] == own_ids[:, None]).astype(f32)
    chunks = n_exp // 2
    grad_ffn_parts = [None] * n_exp
    logit_chunks = [None] * chunks
    kept = [None]

    def run_chunk(i, slots):
        a, b = (n_exp - i) % n_exp, i + 1
        chunk = jnp.concatenate([slots[a], slots[b]], axis=0)
        grad_chunk, *kept_now, logit_chunks[i] = expert_chunk(
            i,
            chunks,
            num_experts,
            chips.places,
            chunk,
            back_hidden,
            chosen_all,
            select,
            router_wide,
            gu_blocks,
            kept[0],
        )
        kept[0] = tuple(kept_now)
        grad_ffn_parts[a], grad_ffn_parts[b] = grad_chunk[:tok_rows], grad_chunk[tok_rows:]
        return logit_chunks[i]

    ffn_slots = ring.gather(ffn_in, lambda s, slots: run_chunk(s - 1, slots), back_hidden, 3)
    run_chunk(chunks - 1, ffn_slots)
    run_chunk(chunks - 2, ffn_slots)
    ffn_all = in_order(ffn_slots)
    grad_pre, gated_act = kept[0]
    logit_low = jnp.concatenate(logit_chunks, axis=0)
    router_part = dot(ffn_all, logit_low, ((0,), (0,)))[:, :num_experts]

    steps = n_dp // 2
    gu_cols, down_cols = experts_dev * 2 * ff_dev, experts_dev * ff_dev
    ffn_peer, grad_peer = chips.other_core(ffn_all), chips.other_core(grad_top_all)
    pre_away = [
        grad_pre[:, (steps + s) * gu_cols : (steps + s + 1) * gu_cols] for s in range(steps)
    ]
    act_away = [
        lax.dynamic_slice_in_dim(gated_act, chips.places[2 * s + 1] * down_cols, down_cols, 1)
        for s in range(steps)
    ]
    away_peer = chips.other_core(jnp.concatenate(pre_away + act_away, axis=1))
    terms = [None] * steps
    jobs = list(range(steps - 1, -1, -1))

    def next_term(wait):
        if not jobs:
            return None
        s = jobs.pop(0)
        terms[s] = pair_grad(
            s,
            chips.places[2 * s : 2 * s + 1],
            grad_pre,
            away_peer,
            gu_cols,
            ffn_all,
            ffn_peer,
            gated_act,
            steps * gu_cols // down_cols,
            down_cols,
            grad_top_all,
            grad_peer,
            wait,
            bf16,
        )
        return terms[s]

    grad_ffn = ring.reduce(
        grad_ffn_parts, lambda s, x: next_term(x) if s == 2 else None
    )

    grad_top = out_grad.astype(f32)
    ffn_gain_part = jnp.sum(ffn_normed * grad_ffn, axis=0)
    grad_mixed = grad_top + norm_back(grad_ffn, ffn_gain, ffn_normed, ffn_scale)
    moe_made = []

    def in_gather(s, slots):
        if s == 1:
            moe_made.append(product(gated_act, down_all, slots[1]))
            return moe_made[0]
        return next_term(slots[s])

    branch_slots = ring.gather(
        grad_mixed.astype(bf16), in_gather
    )
    while jobs:
        next_term(branch_slots[n_exp // 2])
    all_terms = [terms[0]] + [chips.to_ahead(terms[s], s) for s in range(1, steps)]
    grad_rows = in_order(branch_slots)
    moe_parts = slots_of(moe_made[0])
    moe_parts[n_exp // 2] = tie(moe_parts[n_exp // 2], branch_slots[2])
    moe_steps = {}
    moe = ring.reduce(moe_parts, moe_steps.__setitem__)
    output = mixed + moe

    grad_attended = dot(grad_rows, out_full, ((1,), (0,))).astype(bf16)
    grad_attended = grad_attended.reshape(rows, heads, head_dim).transpose(1, 0, 2)
    grad_query, grad_key, grad_value = attend_back(
        query, key, value, grad_attended, segment, log_sums, scaling
    )
    grad_query = rotate_back(grad_query, cos_rows, sin_rows)
    grad_key = rotate_back(grad_key, cos_rows, sin_rows)
    grad_query = tie(grad_query, moe_steps[2])
    query_gain_part = jnp.sum(query_normed * grad_query, axis=(0, 1))
    key_gain_part = jnp.sum(key_normed * grad_key, axis=(0, 1))
    grad_query = norm_back(grad_query, query_gain, query_normed, query_scale)
    grad_key = norm_back(grad_key, key_gain, key_normed, key_scale)
    grad_proj = (
        jnp.stack([grad_query, grad_key, grad_value], axis=0)
        .astype(bf16)
        .transpose(0, 2, 1, 3)
        .reshape(3, rows, local_width)
    )
    features_part = jnp.einsum("ctf,cdf->td", grad_proj, qkv_full, preferred_element_type=f32)
    attn_gain_part = jnp.sum(attn_normed * features_part, axis=0)
    squares = jnp.stack([jnp.sum(output * output), jnp.sum(branch * branch), jnp.sum(moe * moe)])
    wide = all_sum(jnp.concatenate([router_part.T, ffn_gain_part[None]], axis=0))
    small = all_sum(
        jnp.concatenate(
            [attn_gain_part, query_gain_part, key_gain_part, jnp.pad(squares, (0, 125))]
        ).reshape(-1, 128)
    ).reshape(-1)
    weight_grads = []

    def at_end(s, x):
        if s == n_exp // 2 - 1:
            weight_grads.extend(finish(all_terms, experts_dev, ff_dev, x))
            return weight_grads[1]
        return wide if s == 1 else None

    grad_features = ring.reduce(slots_of(features_part), at_end, (small,))
    grad_proj = tie(grad_proj, features_part)
    qkv_term = jnp.einsum("td,ctf->cdf", features, grad_proj, preferred_element_type=f32)
    out_term = dot(grad_rows, attended, ((0,), (0,)))
    attn_sums = lax.psum_scatter(
        jnp.concatenate([qkv_term, out_term[None]], axis=0).astype(bf16),
        "dp",
        scatter_dimension=1,
        tiled=True,
    ).astype(f32)
    own_scale = rms_scale(states)
    input_grad = grad_mixed + norm_back(grad_features, attn_gain, states * own_scale, own_scale)

    stream_rms = jnp.sqrt(small[width + 2 * head_dim :][:3] / (rows * n_dp * width))
    return (
        output.astype(bf16),
        input_grad.astype(bf16),
        small[:width],
        attn_sums[:3].transpose(1, 0, 2),
        attn_sums[3],
        small[width : width + head_dim],
        small[width + head_dim : width + 2 * head_dim],
        wide[num_experts],
        wide[:num_experts].T,
        *weight_grads,
        stream_rms,
    )


def solution(mesh):
    in_specs = (
        P(("dp", "expert"), None),
        P(("dp", "expert"), None),
        P("dp", None),
        P("dp", None),
        P(("dp", "expert"), None),
        P(),
        P("dp", None, "expert"),
        P("dp", "expert"),
        P(),
        P(),
        P(),
        P(),
        P("dp", "expert", None, None),
        P("dp", "expert", None),
    )
    out_specs = (
        P(("dp", "expert"), None),
        P(("dp", "expert"), None),
        P(),
        P("dp", None, "expert"),
        P("dp", "expert"),
        P(),
        P(),
        P(),
        P(),
        P("dp", "expert", None, None),
        P("dp", "expert", None),
        P(),
    )
    return jax.shard_map(
        on_device, mesh=mesh, in_specs=in_specs, out_specs=out_specs, check_vma=False
    )
```

```python
import functools

import jax
import jax.numpy as jnp
from jax import lax
from jax.experimental import pallas as pl
from jax.experimental.pallas import tpu as pltpu
from jax.sharding import PartitionSpec as P

eps_norm = 1e-06
rope_base = 10000.0
big_negative = -1e30
bf16 = jnp.bfloat16
f32 = jnp.float32


def expert_ring(count):
    nz = 4
    ny = count // nz
    walk = [(z, 0) for z in range(nz)]
    for z in range(nz - 1, -1, -1):
        ys = range(1, ny) if (nz - 1 - z) % 2 == 0 else range(ny - 1, 0, -1)
        walk += [(z, y) for y in ys]
    return [z * ny + y for z, y in walk]


def dot(a, b, dims):
    return lax.dot_general(a, b, (dims, ((), ())), preferred_element_type=f32)


class Ring:
    def __init__(self, count):
        self.count = count
        self.order = expert_ring(count)
        n = count
        self.down = [(self.order[(i + 1) % n], self.order[i]) for i in range(n)]
        self.up = [(self.order[i], self.order[(i + 1) % n]) for i in range(n)]
        place = [0] * n
        for i, m in enumerate(self.order):
            place[m] = i
        me = lax.axis_index("expert")
        self.me = me
        self.pos = jnp.array(place, jnp.int32)[me]
        ids = jnp.arange(n, dtype=jnp.int32)
        places = (self.pos + jnp.array(slot_order(n), jnp.int32)) % n
        table = jnp.array(self.order, jnp.int32)
        self.members = jnp.sum(jnp.where(places[:, None] == ids[None, :], table[None, :], 0), axis=1)

    def send(self, x, way):
        return lax.ppermute(x, "expert", way)

    def gather(self, own, arrived=None, first=None, lag=2):
        n = self.count
        half = own.shape[0] // 2
        slots = [None] * n
        slots[0] = own
        ahead = behind = own
        given = {}
        for s in range(1, n // 2 + 1):
            for done in [given.get(s - lag), first if s == 2 else None]:
                if done is not None:
                    ahead, behind = tie(ahead, done), tie(behind, done)
            if s == n // 2:
                break
            ahead = self.send(ahead, self.down)
            behind = self.send(behind, self.up)
            slots[s] = ahead
            slots[n - s] = behind
            if arrived is not None and s <= n // 2 - 2:
                given[s] = arrived(s, slots)
        slots[n // 2] = jnp.concatenate(
            [self.send(ahead[:half], self.down), self.send(behind[half:], self.up)], axis=0
        )
        return slots

    def reduce(self, parts, sent=None, last=()):
        n = self.count
        far = parts[n // 2]
        half = far.shape[0] // 2
        fwd, back = far[:half].astype(bf16), far[half:].astype(bf16)
        wait = None
        for s in range(n // 2 - 1, -1, -1):
            fwd = self.send(fwd, self.up)
            back = self.send(back, self.down)
            if s == 0:
                break
            a, b = parts[s].astype(f32), parts[n - s].astype(f32)
            if wait is not None:
                a = tie(a, wait)
            wait = None
            if s == n // 2 - 1:
                fwd = jnp.concatenate([a[:half] + fwd.astype(f32), a[half:]], axis=0)
                back = jnp.concatenate([b[:half], b[half:] + back.astype(f32)], axis=0)
            else:
                fwd = a + fwd.astype(f32)
                back = b + back.astype(f32)
            fwd, back = fwd.astype(bf16), back.astype(bf16)
            wait = sent(s, back) if sent is not None else None
        total = parts[0].astype(f32)
        for ahead_of in (wait, *last):
            if ahead_of is not None:
                total = tie(total, ahead_of)
        return total + fwd.astype(f32) + back.astype(f32)


class Chips:
    def __init__(self, count):
        self.steps = count // 2
        me = lax.axis_index("dp")
        self.places = jnp.stack(
            [
                ((me // 2 + b // 2) % self.steps) * 2 + (me % 2 + b % 2) % 2
                for b in range(count)
            ]
        ).astype(jnp.int32)
        self.swap = [(i, i ^ 1) for i in range(count)]

    def other_core(self, x):
        return lax.ppermute(x, "dp", self.swap)

    def from_ahead(self, x, step):
        n = self.steps
        return lax.ppermute(
            x, "dp", [(((i // 2 + step) % n) * 2 + i % 2, i) for i in range(2 * n)]
        )

    def to_ahead(self, x, step):
        n = self.steps
        return lax.ppermute(
            x, "dp", [(i, ((i // 2 + step) % n) * 2 + i % 2) for i in range(2 * n)]
        )

    def first_half(self, own):
        ahead = [self.from_ahead(own, step) for step in range(1, self.steps)]
        return [own, self.other_core(own), *ahead]

    def second_half(self, blocks, wait):
        out = blocks[:2]
        for block in blocks[2:]:
            block = tie(block, wait)
            out += [block, self.other_core(block)]
        return out


def block_at(step, steps, experts_dev):
    block = step // experts_dev
    half = steps // experts_dev // 2
    return 2 * (block % half) + block // half


def expert_kernel(
    steps,
    num_experts,
    places,
    f_ref,
    h_ref,
    mask_ref,
    sel_ref,
    wr_ref,
    *refs,
):
    w_refs = refs[: steps // sel_ref.shape[0]]
    gc_ref, gp_ref, ga_ref, gl_ref, acc, router, gate_sums, held, sems = refs[-9:]
    step = pl.program_id(0)
    experts_dev = sel_ref.shape[0]
    ff_tile = h_ref.shape[1]
    rows_in = f_ref[...]
    now = lax.rem(step, 2)

    def fetch(target):
        for j in range(steps):

            @pl.when(target == j)
            def _():
                pltpu.make_async_copy(
                    w_refs[block_at(j, steps, experts_dev)].at[j % experts_dev],
                    held.at[j % 2],
                    sems.at[j % 2],
                ).start()

    @pl.when(step == 0)
    def _():
        fetch(step)

    fetch(step + 1)

    @pl.when(step == 0)
    def _():
        logits = jnp.dot(rows_in, wr_ref[...], preferred_element_type=f32)
        lane = lax.broadcasted_iota(jnp.int32, logits.shape, 1)
        logits = jnp.where(lane < num_experts, logits, big_negative)
        exps = jnp.exp(logits - jnp.max(logits, axis=-1, keepdims=True))
        router[...] = exps / jnp.sum(exps, axis=-1, keepdims=True)
        gate_sums[...] = jnp.zeros_like(gate_sums)
        acc[...] = jnp.zeros_like(acc)

    lanes = sel_ref[pl.ds(step % experts_dev, 1), :] * mask_ref[...].astype(f32)
    gate = jnp.sum(router[...] * lanes, axis=-1, keepdims=True)
    pltpu.make_async_copy(w_refs[0].at[0], held.at[now], sems.at[now]).wait()
    weight_gate, weight_up = held[now, 0], held[now, 1]
    gate_pre = dot(rows_in, weight_gate, ((1,), (1,)))
    up_pre = dot(rows_in, weight_up, ((1,), (1,)))
    back_hidden = h_ref[...]
    sigmoid_gate = 1.0 / (1.0 + jnp.exp(-gate_pre))
    silu_gate = gate_pre * sigmoid_gate
    act = silu_gate * up_pre
    gate_sums[...] += lanes * jnp.sum(act * back_hidden, axis=-1, keepdims=True)
    grad_hidden = back_hidden * gate
    grad_gate = grad_hidden * up_pre * sigmoid_gate * (1.0 + gate_pre * (1.0 - sigmoid_gate))
    grad_gate = grad_gate.astype(bf16)
    grad_up = (grad_hidden * silu_gate).astype(bf16)
    gp_ref[:, :ff_tile] = grad_gate
    gp_ref[:, ff_tile:] = grad_up
    ga_ref[...] = (act * gate).astype(bf16)
    acc[...] += jnp.dot(grad_gate, weight_gate, preferred_element_type=f32) + jnp.dot(
        grad_up, weight_up, preferred_element_type=f32
    )

    @pl.when(step == steps - 1)
    def _():
        sums = gate_sums[...]
        inner = jnp.sum(router[...] * sums, axis=-1, keepdims=True)
        grad_logits = (router[...] * (sums - inner)).astype(bf16)
        gl_ref[...] = grad_logits
        total = acc[...] + dot(grad_logits, wr_ref[...], ((1,), (1,)))
        gc_ref[...] = total.astype(bf16)


def expert_chunk(
    index, chunks, num_experts, places, f, hidden, mask, select, router, weights, kept
):
    experts_dev, _, ff_tile, width = weights[0].shape
    steps = len(weights) * experts_dev
    rows = f.shape[0]
    whole = pl.BlockSpec(memory_space=pltpu.VMEM)
    apart = pl.BlockSpec(memory_space=pl.ANY)

    def placed(j, places):
        return (index, places[block_at(j, steps, experts_dev)] * experts_dev + j % experts_dev)

    in_specs = [
        whole,
        pl.BlockSpec((rows, ff_tile), placed),
        pl.BlockSpec((rows, 128), lambda j, places: (index, 0)),
        whole,
        whole,
    ] + [apart] * len(weights)
    args = [places, f, hidden, mask, select, router, *weights]
    aliases = {}
    if kept is not None:
        in_specs += [apart] * 2
        aliases = {len(args) + i: 1 + i for i in range(2)}
        args += list(kept)
    total = rows * chunks
    return pl.pallas_call(
        functools.partial(expert_kernel, steps, num_experts),
        grid_spec=pltpu.PrefetchScalarGridSpec(
            num_scalar_prefetch=1,
            grid=(steps,),
            in_specs=in_specs,
            out_specs=[
                pl.BlockSpec((rows, width), lambda j, places: (0, 0)),
                pl.BlockSpec((rows, 2 * ff_tile), lambda j, places: (index, j)),
                pl.BlockSpec((rows, ff_tile), placed),
                pl.BlockSpec((rows, 128), lambda j, places: (0, 0)),
            ],
            scratch_shapes=[
                pltpu.VMEM((rows, width), f32),
                pltpu.VMEM((rows, 128), f32),
                pltpu.VMEM((rows, 128), f32),
                pltpu.VMEM((2, 2, ff_tile, width), bf16),
                pltpu.SemaphoreType.DMA((2,)),
            ],
        ),
        out_shape=[
            jax.ShapeDtypeStruct((rows, width), bf16),
            jax.ShapeDtypeStruct((total, 2 * ff_tile * steps), bf16),
            jax.ShapeDtypeStruct((total, ff_tile * steps), bf16),
            jax.ShapeDtypeStruct((rows, 128), bf16),
        ],
        input_output_aliases=aliases,
        compiler_params=pltpu.CompilerParams(vmem_limit_bytes=40 << 20),
        cost_estimate=pl.CostEstimate(
            flops=8 * rows * ff_tile * steps * width,
            bytes_accessed=4 * ff_tile * steps * width,
            transcendentals=0,
        ),
    )(*args)


def finish_kernel(experts_dev, own_ref, *refs):
    gu_ref, down_ref = refs[-2:]
    for e in range(experts_dev):
        for k in range(3):
            block = 2 * e + k if k < 2 else 2 * experts_dev + e
            total = own_ref[block].astype(f32)
            for ref in refs[:-3]:
                total = total + ref[block].astype(f32)
            if k < 2:
                gu_ref[:, e, k, :] = total
            else:
                down_ref[:, e, :] = total


def finish(terms, experts_dev, ff_dev, wait):
    width = terms[0].shape[1]
    tile = 32
    blocks = 3 * experts_dev
    return pl.pallas_call(
        functools.partial(finish_kernel, experts_dev),
        grid=(ff_dev // tile,),
        in_specs=[pl.BlockSpec((blocks, tile, width), lambda i: (0, i, 0))] * len(terms)
        + [pl.BlockSpec(memory_space=pl.ANY)],
        out_specs=[
            pl.BlockSpec((tile, experts_dev, 2, width), lambda i: (i, 0, 0, 0)),
            pl.BlockSpec((tile, experts_dev, width), lambda i: (i, 0, 0)),
        ],
        out_shape=[
            jax.ShapeDtypeStruct((ff_dev, experts_dev, 2, width), f32),
            jax.ShapeDtypeStruct((ff_dev, experts_dev, width), f32),
        ],
        compiler_params=pltpu.CompilerParams(vmem_limit_bytes=40 << 20),
        cost_estimate=pl.CostEstimate(
            flops=0, bytes_accessed=8 * blocks * ff_dev * width, transcendentals=0
        ),
    )(*[t.reshape(blocks, ff_dev, width) for t in terms], wait)


def product_kernel(a_ref, b_ref, _, o_ref):
    o_ref[...] = jnp.dot(a_ref[...], b_ref[...], preferred_element_type=f32).astype(bf16)


def product(a, b, wait):
    rows, depth = a.shape
    width = b.shape[1]
    tile = min(512, rows)
    return pl.pallas_call(
        product_kernel,
        grid=(rows // tile,),
        in_specs=[
            pl.BlockSpec((tile, depth), lambda i: (i, 0)),
            pl.BlockSpec(memory_space=pltpu.VMEM),
            pl.BlockSpec(memory_space=pl.ANY),
        ],
        out_specs=pl.BlockSpec((tile, width), lambda i: (i, 0)),
        out_shape=jax.ShapeDtypeStruct((rows, width), bf16),
        compiler_params=pltpu.CompilerParams(vmem_limit_bytes=40 << 20),
        cost_estimate=pl.CostEstimate(
            flops=2 * rows * depth * width, bytes_accessed=4 * rows * depth, transcendentals=0
        ),
    )(a, b, wait)


def pair_kernel(first, block, a_ref, ap_ref, b_ref, bp_ref, x_ref, xp_ref, y_ref, yp_ref, _, o_ref):
    def product(own, peer, rows, rows_peer):
        total = dot(own[...], rows[...], ((0,), (0,))) + dot(peer[...], rows_peer[...], ((0,), (0,)))
        o_ref[...] = total.astype(o_ref.dtype)

    @pl.when(pl.program_id(0) < first)
    def _():
        product(a_ref, ap_ref, x_ref, xp_ref)

    @pl.when(pl.program_id(0) >= first)
    def _():
        product(b_ref, bp_ref, y_ref, yp_ref)


def pair_grad(
    step, block, a, peer, a_cols, x, x_peer, b, b_first, b_cols, y, y_peer, wait, dtype
):
    rows, width = x.shape
    tile = min(256, b_cols)
    first, second = a_cols // tile, b_cols // tile
    whole = pl.BlockSpec(memory_space=pltpu.VMEM)

    def a_at(j, block):
        return (0, step * first + jnp.minimum(j, first - 1))

    def b_at(j, block):
        return (0, block[0] * second + jnp.maximum(j - first, 0))

    def bp_at(j, block):
        return (0, (b_first + step) * second + jnp.maximum(j - first, 0))

    return pl.pallas_call(
        functools.partial(pair_kernel, first),
        grid_spec=pltpu.PrefetchScalarGridSpec(
            num_scalar_prefetch=1,
            grid=(first + second,),
            in_specs=[
                pl.BlockSpec((rows, tile), a_at),
                pl.BlockSpec((rows, tile), a_at),
                pl.BlockSpec((rows, tile), b_at),
                pl.BlockSpec((rows, tile), bp_at),
                whole,
                whole,
                whole,
                whole,
                pl.BlockSpec(memory_space=pl.ANY),
            ],
            out_specs=pl.BlockSpec((tile, width), lambda j, block: (j, 0)),
        ),
        out_shape=jax.ShapeDtypeStruct((a_cols + b_cols, width), dtype),
        compiler_params=pltpu.CompilerParams(vmem_limit_bytes=44 << 20),
        cost_estimate=pl.CostEstimate(
            flops=4 * rows * (a_cols + b_cols) * width,
            bytes_accessed=16 * rows * width,
            transcendentals=0,
        ),
    )(block, a, peer, b, peer, x, x_peer, y, y_peer, wait)


def all_sum(x):
    for axis in ("dp", "expert"):
        n = lax.axis_size(axis)
        bit = 1
        while bit < n:
            x = x + lax.ppermute(x, axis, [(i, i ^ bit) for i in range(n)])
            bit *= 2
    return x


def slot_order(n):
    return [k for i in range(n // 2) for k in ((n - i) % n, i + 1)]


def in_order(slots):
    return jnp.concatenate([slots[k] for k in slot_order(len(slots))], axis=0)


def tie(x, other):
    probe = other[(0,) * other.ndim]
    return x + jnp.where(probe == probe, 0.0, 1.0).astype(x.dtype)


def rms_scale(values):
    return lax.rsqrt(jnp.mean(values * values, axis=-1, keepdims=True) + eps_norm)


def norm_back(grad_out, norm_gain, normed, row_scale):
    scaled = grad_out * norm_gain
    inner_mean = jnp.mean(normed * scaled, axis=-1, keepdims=True)
    return row_scale * (scaled - normed * inner_mean)


def seq_layout(lengths, seq_order, places):
    seq_count = lengths.shape[0]
    ids = jnp.arange(seq_count, dtype=jnp.int32)
    picked_seq = seq_order[:, None] == ids[None, :]
    ordered = jnp.sum(jnp.where(picked_seq, lengths[None, :], 0), axis=1)
    upto = ids[:, None] >= ids[None, :]
    seq_ends = jnp.sum(jnp.where(upto, ordered[None, :], 0), axis=1)
    starts = seq_ends - ordered
    segment = jnp.sum((places[:, None] >= seq_ends[None, :]).astype(jnp.int32), axis=1)
    member = segment[:, None] == ids[None, :]
    position = places - jnp.sum(jnp.where(member, starts[None, :], 0), axis=1)
    return (segment, position)


def rope_tables(position, head_dim):
    half_dim = head_dim // 2
    inv_freq = rope_base ** (-(jnp.arange(half_dim, dtype=f32) * 2.0 / head_dim))
    angles = position.astype(f32)[:, None] * inv_freq[None, :]
    return (jnp.cos(angles), jnp.sin(angles))


def rotate(values, cos_rows, sin_rows):
    half_dim = values.shape[-1] // 2
    a, b = values[..., :half_dim], values[..., half_dim:]
    return jnp.concatenate([a * cos_rows - b * sin_rows, b * cos_rows + a * sin_rows], axis=-1)


def rotate_back(grad_out, cos_rows, sin_rows):
    return rotate(grad_out, cos_rows, -sin_rows)


def attend(query, key, value, segment, scaling):
    scores = jnp.einsum("hqd,hkd->hqk", query, key, preferred_element_type=f32) * scaling
    allowed = segment[:, None] == segment[None, :]
    scores = jnp.where(allowed[None], scores, big_negative)
    row_max = jnp.max(scores, axis=-1, keepdims=True)
    exp_scores = jnp.exp(scores - row_max)
    row_sum = jnp.sum(exp_scores, axis=-1, keepdims=True)
    probs = (exp_scores / row_sum).astype(bf16)
    attended = jnp.einsum("hqk,hkd->hqd", probs, value, preferred_element_type=f32)
    return attended, row_max + jnp.log(row_sum)


def attend_back(query, key, value, grad, segment, log_sums, scaling):
    scores = jnp.einsum("hqd,hkd->hqk", query, key, preferred_element_type=f32) * scaling
    allowed = segment[:, None] == segment[None, :]
    scores = jnp.where(allowed[None], scores, big_negative)
    probs = jnp.exp(scores - log_sums)
    grad_probs = jnp.einsum("hqd,hkd->hqk", grad, value, preferred_element_type=f32)
    inner = jnp.sum(probs * grad_probs, axis=-1, keepdims=True)
    grad_scores = (probs * (grad_probs - inner)).astype(bf16)
    grad_query = jnp.einsum("hqk,hkd->hqd", grad_scores, key, preferred_element_type=f32) * scaling
    grad_key = jnp.einsum("hqk,hqd->hkd", grad_scores, query, preferred_element_type=f32) * scaling
    grad_value = jnp.einsum("hqk,hqd->hkd", probs.astype(bf16), grad, preferred_element_type=f32)
    return grad_query, grad_key, grad_value


def on_device(
    hidden_states,
    out_grad,
    seq_lengths,
    seq_order,
    expert_routes,
    attn_gain,
    qkv_weight,
    out_weight,
    query_gain,
    key_gain,
    ffn_gain,
    router_weight,
    expert_gate_up,
    expert_down,
):
    tok_rows, width = hidden_states.shape
    head_dim = query_gain.shape[0]
    ff_dev, experts_dev = expert_gate_up.shape[:2]
    n_dp = lax.axis_size("dp")
    n_exp = lax.axis_size("expert")
    ff = ff_dev * n_dp
    num_experts = experts_dev * n_exp
    scaling = head_dim ** (-0.5)
    ring = Ring(n_exp)
    rows = tok_rows * n_exp

    chips = Chips(n_dp)
    qkv_full = lax.all_gather(qkv_weight.transpose(1, 0, 2), "dp", axis=1, tiled=True)
    out_full = lax.all_gather(out_weight, "dp", axis=0, tiled=True)
    local_width = out_full.shape[1]
    heads = local_width // head_dim

    states_slots = ring.gather(hidden_states)
    states_all = in_order(states_slots).astype(f32)
    attn_scale = rms_scale(states_all)
    attn_normed = states_all * attn_scale
    features = (attn_normed * attn_gain).astype(bf16)

    down_all = lax.all_gather(expert_down.transpose(1, 0, 2), "dp", axis=0)
    down_all = down_all.reshape(n_dp * experts_dev * ff_dev, width)
    gu_blocks = chips.first_half(expert_gate_up.transpose(1, 2, 0, 3))

    expert_ids = jnp.arange(num_experts, dtype=jnp.int32)
    chosen = jnp.any(expert_routes[:, :, None] == expert_ids[None, None, :], axis=1)
    chosen = jnp.pad(chosen.astype(bf16), ((0, 0), (0, 128 - num_experts)))
    sent_grad = jnp.concatenate([out_grad, chosen], axis=1)
    place = (ring.members[:, None] * tok_rows + jnp.arange(tok_rows, dtype=jnp.int32)).reshape(-1)
    segment, position = seq_layout(seq_lengths[0], seq_order[0], place)
    cos_rows, sin_rows = rope_tables(position, head_dim)

    projected = jnp.einsum("td,cdf->ctf", features, qkv_full, preferred_element_type=f32)
    sent_grad = tie(sent_grad, states_slots[n_exp // 2])
    stages = {1: projected}
    grad_slots = ring.gather(sent_grad, lambda s, slots: stages.get(s), lag=1)
    grad_top_all = in_order([g[:, :width] for g in grad_slots])
    chosen_all = in_order([g[:, width:] for g in grad_slots])
    back_hidden = dot(grad_top_all, down_all, ((1,), (1,)))

    head_proj = projected.reshape(3, rows, heads, head_dim).transpose(0, 2, 1, 3)
    query_scale, key_scale = rms_scale(head_proj[0]), rms_scale(head_proj[1])
    query_normed, key_normed = head_proj[0] * query_scale, head_proj[1] * key_scale
    query = rotate(query_normed * query_gain, cos_rows, sin_rows)
    query = tie(query, grad_slots[1]).astype(bf16)
    key = rotate(key_normed * key_gain, cos_rows, sin_rows).astype(bf16)
    value = head_proj[2].astype(bf16)
    attended, log_sums = attend(query, key, value, segment, scaling)
    attended = attended.transpose(1, 0, 2).reshape(rows, local_width)
    attended = tie(attended, grad_slots[2]).astype(bf16)
    branch_part = dot(attended, out_full, ((1,), (1,)))

    def slots_of(x):
        where = slot_order(n_exp)
        return [x[i * tok_rows : (i + 1) * tok_rows] for i in map(where.index, range(n_exp))]

    branch = ring.reduce(slots_of(branch_part))
    states = hidden_states.astype(f32)
    mixed = states + branch
    ffn_scale = rms_scale(mixed)
    ffn_normed = mixed * ffn_scale
    ffn_in = (ffn_normed * ffn_gain).astype(bf16)
    gu_blocks = chips.second_half(gu_blocks, ffn_in)

    router_wide = jnp.pad(router_weight, ((0, 0), (0, 128 - num_experts)))
    lanes = jnp.arange(128, dtype=jnp.int32)
    own_ids = ring.me * experts_dev + jnp.arange(experts_dev, dtype=jnp.int32)
    select = (lanes[None, :] == own_ids[:, None]).astype(f32)
    chunks = n_exp // 2
    grad_ffn_parts = [None] * n_exp
    logit_chunks = [None] * chunks
    kept = [None]

    def run_chunk(i, slots):
        a, b = (n_exp - i) % n_exp, i + 1
        chunk = jnp.concatenate([slots[a], slots[b]], axis=0)
        grad_chunk, *kept_now, logit_chunks[i] = expert_chunk(
            i,
            chunks,
            num_experts,
            chips.places,
            chunk,
            back_hidden,
            chosen_all,
            select,
            router_wide,
            gu_blocks,
            kept[0],
        )
        kept[0] = tuple(kept_now)
        grad_ffn_parts[a], grad_ffn_parts[b] = grad_chunk[:tok_rows], grad_chunk[tok_rows:]
        return logit_chunks[i]

    ffn_slots = ring.gather(ffn_in, lambda s, slots: run_chunk(s - 1, slots), back_hidden, 3)
    run_chunk(chunks - 1, ffn_slots)
    run_chunk(chunks - 2, ffn_slots)
    ffn_all = in_order(ffn_slots)
    grad_pre, gated_act = kept[0]
    logit_low = jnp.concatenate(logit_chunks, axis=0)
    router_part = dot(ffn_all, logit_low, ((0,), (0,)))[:, :num_experts]

    steps = n_dp // 2
    gu_cols, down_cols = experts_dev * 2 * ff_dev, experts_dev * ff_dev
    ffn_peer, grad_peer = chips.other_core(ffn_all), chips.other_core(grad_top_all)
    pre_away = [
        grad_pre[:, (steps + s) * gu_cols : (steps + s + 1) * gu_cols] for s in range(steps)
    ]
    act_away = [
        lax.dynamic_slice_in_dim(gated_act, chips.places[2 * s + 1] * down_cols, down_cols, 1)
        for s in range(steps)
    ]
    away_peer = chips.other_core(jnp.concatenate(pre_away + act_away, axis=1))
    terms = [None] * steps
    jobs = list(range(steps - 1, -1, -1))

    def next_term(wait):
        if not jobs:
            return None
        s = jobs.pop(0)
        terms[s] = pair_grad(
            s,
            chips.places[2 * s : 2 * s + 1],
            grad_pre,
            away_peer,
            gu_cols,
            ffn_all,
            ffn_peer,
            gated_act,
            steps * gu_cols // down_cols,
            down_cols,
            grad_top_all,
            grad_peer,
            wait,
            bf16,
        )
        return terms[s]

    grad_ffn = ring.reduce(
        grad_ffn_parts, lambda s, x: next_term(x) if s == 2 else None
    )

    grad_top = out_grad.astype(f32)
    ffn_gain_part = jnp.sum(ffn_normed * grad_ffn, axis=0)
    grad_mixed = grad_top + norm_back(grad_ffn, ffn_gain, ffn_normed, ffn_scale)
    moe_made = []

    def in_gather(s, slots):
        if s == 1:
            moe_made.append(product(gated_act, down_all, slots[1]))
            return moe_made[0]
        return next_term(slots[s])

    branch_slots = ring.gather(
        grad_mixed.astype(bf16), in_gather
    )
    while jobs:
        next_term(branch_slots[n_exp // 2])
    all_terms = [terms[0]] + [chips.to_ahead(terms[s], s) for s in range(1, steps)]
    grad_rows = in_order(branch_slots)
    moe_parts = slots_of(moe_made[0])
    moe_parts[n_exp // 2] = tie(moe_parts[n_exp // 2], branch_slots[2])
    moe_steps = {}
    moe = ring.reduce(moe_parts, moe_steps.__setitem__)
    output = mixed + moe

    grad_attended = dot(grad_rows, out_full, ((1,), (0,))).astype(bf16)
    grad_attended = grad_attended.reshape(rows, heads, head_dim).transpose(1, 0, 2)
    grad_query, grad_key, grad_value = attend_back(
        query, key, value, grad_attended, segment, log_sums, scaling
    )
    grad_query = rotate_back(grad_query, cos_rows, sin_rows)
    grad_key = rotate_back(grad_key, cos_rows, sin_rows)
    grad_query = tie(grad_query, moe_steps[1])
    query_gain_part = jnp.sum(query_normed * grad_query, axis=(0, 1))
    key_gain_part = jnp.sum(key_normed * grad_key, axis=(0, 1))
    grad_query = norm_back(grad_query, query_gain, query_normed, query_scale)
    grad_key = norm_back(grad_key, key_gain, key_normed, key_scale)
    grad_proj = (
        jnp.stack([grad_query, grad_key, grad_value], axis=0)
        .astype(bf16)
        .transpose(0, 2, 1, 3)
        .reshape(3, rows, local_width)
    )
    features_part = jnp.einsum("ctf,cdf->td", grad_proj, qkv_full, preferred_element_type=f32)
    attn_gain_part = jnp.sum(attn_normed * features_part, axis=0)
    squares = jnp.stack([jnp.sum(output * output), jnp.sum(branch * branch), jnp.sum(moe * moe)])
    wide = all_sum(jnp.concatenate([router_part.T, ffn_gain_part[None]], axis=0))
    small = all_sum(
        jnp.concatenate(
            [attn_gain_part, query_gain_part, key_gain_part, jnp.pad(squares, (0, 125))]
        ).reshape(-1, 128)
    ).reshape(-1)
    weight_grads = []

    def at_end(s, x):
        if s == n_exp // 2 - 1:
            weight_grads.extend(finish(all_terms, experts_dev, ff_dev, x))
            return weight_grads[1]
        return wide if s == 1 else None

    grad_features = ring.reduce(slots_of(features_part), at_end, (small,))
    grad_proj = tie(grad_proj, features_part)
    qkv_term = jnp.einsum("td,ctf->cdf", features, grad_proj, preferred_element_type=f32)
    out_term = dot(grad_rows, attended, ((0,), (0,)))
    attn_sums = lax.psum_scatter(
        jnp.concatenate([qkv_term, out_term[None]], axis=0).astype(bf16),
        "dp",
        scatter_dimension=1,
        tiled=True,
    ).astype(f32)
    own_scale = rms_scale(states)
    input_grad = grad_mixed + norm_back(grad_features, attn_gain, states * own_scale, own_scale)

    stream_rms = jnp.sqrt(small[width + 2 * head_dim :][:3] / (rows * n_dp * width))
    return (
        output.astype(bf16),
        input_grad.astype(bf16),
        small[:width],
        attn_sums[:3].transpose(1, 0, 2),
        attn_sums[3],
        small[width : width + head_dim],
        small[width + head_dim : width + 2 * head_dim],
        wide[num_experts],
        wide[:num_experts].T,
        *weight_grads,
        stream_rms,
    )


def solution(mesh):
    in_specs = (
        P(("dp", "expert"), None),
        P(("dp", "expert"), None),
        P("dp", None),
        P("dp", None),
        P(("dp", "expert"), None),
        P(),
        P("dp", None, "expert"),
        P("dp", "expert"),
        P(),
        P(),
        P(),
        P(),
        P("dp", "expert", None, None),
        P("dp", "expert", None),
    )
    out_specs = (
        P(("dp", "expert"), None),
        P(("dp", "expert"), None),
        P(),
        P("dp", None, "expert"),
        P("dp", "expert"),
        P(),
        P(),
        P(),
        P(),
        P("dp", "expert", None, None),
        P("dp", "expert", None),
        P(),
    )
    return jax.shard_map(
        on_device, mesh=mesh, in_specs=in_specs, out_specs=out_specs, check_vma=False
    )
```
